256 devices in a mesh: dp: 16 (over y, z_lo), vocab: 16 (over z_hi, x, core).
Axes of the slice: x: 4, y: 4, z: 8 (z_hi: 2, z_lo: 4; z = z_hi * 4 + z_lo), core: 2. Of those that a mesh axis runs over, the one named last changes fastest.
Arguments:
- grad_parts: bfloat16 [16, 16384, 4608], P('dp', 'vocab')
- embedding: float32 [16384, 4608], P('vocab', 'dp'), may hold values from -6 to 6
- stat_prev: float32 [16, 288, 288], P('dp'), as said below
- row_flags: int32 [16384], P('vocab'), may hold values 0 or 1
Outputs:
- updated: float32 [16384, 4608], P('vocab', 'dp')
- statistics: float32 [16, 288, 288], P('dp')
- roots: float32 [16, 288, 288], P('dp', 'vocab')
The draws below stay inside these ranges and needn't reach their ends.
Inputs may be any that keep to these rules, and one draw needn't show every extreme that they name: `stat_prev`: each block is symmetric positive definite.
All inputs are finite; a program needn't handle non-finite values. No bound on the sum of `row_flags` on one device may be relied on, other than what follows from the above.
Results may differ from the reference program's by a relative error of at most 0.0003.
Values sent between devices are 32-bit elements; how exact they have to be, the bound alone decides.
No kernel may reach another device: no remote copies, remote signals or barrier semaphores. Data moves between devices by JAX's collectives and lax.ppermute only.
A program may use at most 128 MiB of HBM per device.

```python
import math
import jax
import jax.numpy as jnp
from jax import lax

D = 4608
BLOCK = 288
ITERS = 2
VOCAB = 16384
BLOCKS = 16
SOURCES = 16


def draw_grad_parts(key, part):
    key = jax.random.fold_in(key, 11)
    keys = jax.random.split(key, 3)
    row_place = jnp.arange(VOCAB, dtype=jnp.float32) / VOCAB
    col_place = jnp.arange(D, dtype=jnp.float32) / D
    row_jitter = jnp.exp(jax.random.uniform(keys[0], (VOCAB,), minval=math.log(0.3), maxval=math.log(3.0)))
    col_jitter = jnp.exp(jax.random.uniform(keys[1], (D,), minval=math.log(0.3), maxval=math.log(3.0)))
    spread = 3.0
    noise = jax.random.normal(keys[2], (SOURCES, VOCAB, D))
    mixed = (noise + 0.6 * jnp.roll(noise, 1, axis=2) + 0.3 * jnp.roll(noise, 5, axis=2)) * 0.8304548
    row_scale = row_jitter * jnp.power(spread, row_place)
    col_scale = col_jitter * jnp.power(spread, col_place)
    values = mixed * row_scale[None, :, None] * col_scale[None, None, :] / jnp.sqrt(1.0 * VOCAB * SOURCES)
    return values.astype(jnp.bfloat16)


def draw_stat_prev(key, part):
    key = jax.random.fold_in(key, 23)
    place_key, scale_key, diag_key = jax.random.split(key, 3)
    place = jax.random.uniform(place_key, (BLOCKS, BLOCK))
    reach = 6.0 / BLOCK
    scales = jnp.exp(jax.random.uniform(scale_key, (BLOCKS, BLOCK), minval=0.0, maxval=math.log(4.0)))
    diagonal = jax.random.uniform(diag_key, (BLOCKS, BLOCK), minval=1.0, maxval=3.0)
    distance = jnp.abs(place[:, :, None] - place[:, None, :])
    kernel = 2.0 * (scales[:, :, None] * scales[:, None, :]) * jnp.exp(-distance / reach)
    identity = jnp.eye(BLOCK, dtype=jnp.float32)[None]
    result = kernel + identity * diagonal[:, :, None]
    return result.astype(jnp.float32)


def touch_ends(drawn, own_key, smallest, high):
    shape = drawn.shape
    index_at = [jax.random.randint(jax.random.fold_in(own_key, axis), (), 0, shape[axis]) for axis in range(len(shape))]
    drawn = drawn.at[tuple(index_at)].set(smallest)
    longest = shape.index(max(shape))
    index_at[longest] = (index_at[longest] + 1) % shape[longest]
    return drawn.at[tuple(index_at)].set(high)


def shard_levels(own_key, shape, cuts, smallest, high):
    def one(dim, blocks):
        draws = jax.random.uniform(jax.random.fold_in(jax.random.fold_in(own_key, 6), dim), (blocks,), jnp.float32, smallest / len(cuts), high / len(cuts))
        return jnp.repeat(jnp.exp(draws), shape[dim] // blocks).reshape((-1,) + (1,) * (len(shape) - dim - 1))

    factor_of = one(*cuts[0])
    for cut in cuts[1:]:
        factor_of = factor_of * one(*cut)
    return factor_of


def centred(stream_key, extent, deviation, most, cuts=(), held_as=jnp.bfloat16):
    loudness = shard_levels(stream_key, extent, cuts, -0.22, 0.18) if cuts else 1.0
    values = jax.random.normal(stream_key, extent, jnp.float32) * deviation * loudness
    return jnp.minimum(jnp.maximum(values, -most), most).astype(held_as)


def setup_inputs(seed: int = 0) -> dict:
    arg_keys = jax.random.split(jax.random.key(seed), 5)
    return {
        "grad_parts": draw_grad_parts(jax.random.fold_in(arg_keys[4], 71), 0),
        "embedding": centred(arg_keys[1], (VOCAB, D), 1.0, 6.0, ((0, 16), (1, 16)), jnp.float32),
        "stat_prev": draw_stat_prev(jax.random.fold_in(arg_keys[4], 71), 0),
        "row_flags": touch_ends((jax.random.randint(arg_keys[3], (VOCAB,), 0, 8) < 7).astype(jnp.int32), jax.random.fold_in(arg_keys[3], 1), 0, 1),
    }


stat_decay = 0.8
learn_rate = 0.5
weight_decay = 0.1
rms_epsilon = 1e-06
start_gain = 2.5
highest = lax.Precision.HIGHEST

def newton_root(statistic):
    norm_scale = jnp.sqrt(jnp.sum(statistic * statistic))
    identity = jnp.eye(BLOCK, dtype=jnp.float32)
    normed = start_gain * statistic / norm_scale
    inverse_root = identity * (start_gain / norm_scale) ** 0.25
    for iteration in range(ITERS):
        newton_step = (5.0 * identity - normed) / 4.0
        inverse_root = jnp.dot(inverse_root, newton_step, precision=highest)
        if iteration + 1 < ITERS:
            squared = jnp.dot(newton_step, newton_step, precision=highest)
            fourth = jnp.dot(squared, squared, precision=highest)
            normed = jnp.dot(fourth, normed, precision=highest)
    return inverse_root

def reference(grad_parts, embedding, stat_prev, row_flags):

    def accumulate(index, total):
        return total + lax.dynamic_index_in_dim(grad_parts, index, 0, keepdims=False).astype(jnp.float32)
    grad_total = lax.fori_loop(0, SOURCES, accumulate, jnp.zeros((VOCAB, D), jnp.float32))
    live_mask = (row_flags > 0).astype(jnp.float32)[:, None]
    live_grad = grad_total * live_mask
    block_cols = jnp.transpose(live_grad.reshape(VOCAB, BLOCKS, BLOCK), (1, 0, 2))

    def per_block(inputs):
        columns, previous = inputs
        gram_sum = jnp.dot(columns.T, columns, precision=highest)
        statistic = stat_decay * previous + (1.0 - stat_decay) * gram_sum
        inverse_root = newton_root(statistic)
        moved = jnp.dot(columns, inverse_root, precision=highest)
        return (statistic, inverse_root, moved)
    statistics, roots, moved_blocks = lax.map(per_block, (block_cols, stat_prev))
    direction = jnp.transpose(moved_blocks, (1, 0, 2)).reshape(VOCAB, D)
    squares = jnp.sum(direction * direction)
    root_mean = jnp.sqrt(squares / (VOCAB * D) + rms_epsilon)
    stepped = (1.0 - learn_rate * weight_decay) * embedding - learn_rate * direction / root_mean
    updated = jnp.where(live_mask > 0, stepped, embedding)
    return (updated, statistics, roots)
```

```python
import jax
import jax.numpy as jnp
from jax import lax
from jax.experimental import pallas as pl
from jax.experimental.pallas import tpu as pltpu
from jax.sharding import PartitionSpec as P

BLOCK = 288
HALF = 144
SLICES = (256, 256, 256, 128, 128)

stat_decay = 0.8
learn_rate = 0.5
weight_decay = 0.1
rms_epsilon = 1e-06
start_gain = 2.5
f32 = jnp.float32
bf16 = jnp.bfloat16

ANY_T = (((1,), (1,)), ((), ()))
MUL = (((1,), (0,)), ((), ()))


def params(mib):
    return pltpu.CompilerParams(vmem_limit_bytes=mib * 2**20)


def cost(flops, moved):
    return pl.CostEstimate(flops=int(flops), bytes_accessed=int(moved), transcendentals=0)


def vm():
    return pl.BlockSpec(memory_space=pltpu.VMEM)


def sm():
    return pl.BlockSpec(memory_space=pltpu.SMEM)


def y_move(step):
    return [(y * 4 + z, ((y + step) % 4) * 4 + z) for y in range(4) for z in range(4)]


def z_flip(mask):
    return [(y * 4 + z, y * 4 + (z ^ mask)) for y in range(4) for z in range(4)]


def v_move(dh, dx, dc):
    pairs = []
    for h in range(2):
        for x in range(4):
            for c in range(2):
                to = (((h + dh) % 2) * 4 + (x + dx) % 4) * 2 + (c + dc) % 2
                pairs.append(((h * 4 + x) * 2 + c, to))
    return pairs


def split(value):
    high = value.astype(bf16)
    low = (value - high.astype(f32)).astype(bf16)
    return high, low


def dot3(left, right, dims):
    (a, b), (c, d) = left, right
    one = lambda p, q: lax.dot_general(p, q, dims, preferred_element_type=f32)
    return one(a, c) + (one(a, d) + one(b, c))


def prep_kernel(at_ref, grad_ref, first_ref, second_ref):
    outs = (first_ref, second_ref)
    for tile in range(9):
        turned = grad_ref[:, tile * 128 : (tile + 1) * 128].astype(f32).T
        place = tile * 128
        while place < (tile + 1) * 128:
            half = place // HALF
            stop = min((half + 1) * HALF, (tile + 1) * 128)
            outs[half % 2][half // 2, place - half * HALF : stop - half * HALF, :] = turned[
                place - tile * 128 : stop - tile * 128, :
            ]
            place = stop


def prep(grad, where, start, rows):
    part = jax.ShapeDtypeStruct((4, HALF, rows), f32)
    spec = pl.BlockSpec((4, HALF, rows), lambda i, at: (0, 0, 0))
    return pl.pallas_call(
        prep_kernel,
        grid_spec=pltpu.PrefetchScalarGridSpec(
            num_scalar_prefetch=1,
            grid=(1,),
            in_specs=[pl.BlockSpec((rows, 1152), lambda i, at: (start // rows, at[0]))],
            out_specs=[spec, spec],
        ),
        out_shape=[part, part],
        compiler_params=params(32),
        cost_estimate=cost(0, rows * 1152 * 16),
        name="prep",
    )(where, grad)


def cut_kernel(z_ref, a0, a1, a2, b0, b1, b2, *outs):
    for mask in range(4):
        at = z_ref[mask]
        outs[mask][0:HALF, :] = a0[at] + (a1[at] + a2[at])
        outs[mask][HALF:BLOCK, :] = b0[at] + (b1[at] + b2[at])


def cut(z_at, parts, rows):
    return pl.pallas_call(
        cut_kernel,
        in_specs=[sm()] + [vm()] * 6,
        out_specs=[vm()] * 4,
        out_shape=[jax.ShapeDtypeStruct((BLOCK, rows), f32)] * 4,
        compiler_params=params(32),
        cost_estimate=cost(1152 * rows * 2, 1152 * rows * 16),
        name="cut",
    )(z_at, *parts)


def pack(full, ref):
    ref[0:128, :] = full[0:128, 0:128]
    ref[128:256, :] = full[0:128, 128:256]
    ref[256:384, :] = full[128:256, 128:256]
    ref[384:416, :] = full[256:288, 0:128]
    ref[416:448, :] = full[256:288, 128:256]
    ref[448:480, 0:32] = full[256:288, 256:288]


def finish_kernel(mask_ref, p0, p1, p2, p3, *refs):
    prior, (live_ref, gram_ref) = refs[:-2], refs[-2:]
    live = ((p0[...] + p1[...]) + (p2[...] + p3[...])) * mask_ref[...]
    live_ref[...] = live
    pair = split(live)
    gram = dot3(pair, pair, ANY_T)
    gram_ref[...] = gram + prior[0][...] if prior else gram


def finish(mask, parts, prior, rows):
    prior = [] if prior is None else [prior]
    return pl.pallas_call(
        finish_kernel,
        in_specs=[vm()] * (5 + len(prior)),
        out_specs=[vm()] * 2,
        out_shape=[
            jax.ShapeDtypeStruct((BLOCK, rows), f32),
            jax.ShapeDtypeStruct((BLOCK, BLOCK), f32),
        ],
        compiler_params=params(32),
        cost_estimate=cost(6 * BLOCK * BLOCK * rows, BLOCK * rows * 24),
        name="finish",
    )(mask, *parts, *prior)


def last_kernel(mask_ref, core_ref, p0, p1, p2, p3, prior, live_ref, keep_ref, send_ref, packed):
    live = ((p0[...] + p1[...]) + (p2[...] + p3[...])) * mask_ref[...]
    live_ref[...] = live
    pair = split(live)
    packed[...] = jnp.zeros_like(packed)
    pack(dot3(pair, pair, ANY_T) + prior[...], packed)
    mine = pl.multiple_of(core_ref[0] * 256, 256)
    keep_ref[...] = packed[pl.ds(mine, 256), :]
    send_ref[...] = packed[pl.ds(256 - mine, 256), :]


def last(mask, core, parts, prior, rows):
    return pl.pallas_call(
        last_kernel,
        in_specs=[vm(), sm()] + [vm()] * 5,
        out_specs=[vm()] * 3,
        out_shape=[
            jax.ShapeDtypeStruct((BLOCK, rows), f32),
            jax.ShapeDtypeStruct((256, 128), f32),
            jax.ShapeDtypeStruct((256, 128), f32),
        ],
        scratch_shapes=[pltpu.VMEM((512, 128), f32)],
        compiler_params=params(32),
        cost_estimate=cost(6 * BLOCK * BLOCK * rows, BLOCK * rows * 24),
        name="last",
    )(mask, core, *parts, prior)


def quarter_kernel(x_ref, keep, came, *outs):
    for step in range(4):
        at = pl.ds(pl.multiple_of(x_ref[step] * 64, 64), 64)
        outs[step][...] = keep[at, :] + came[at, :]


def quarter(x_at, keep, came):
    return pl.pallas_call(
        quarter_kernel,
        in_specs=[sm(), vm(), vm()],
        out_specs=[vm()] * 4,
        out_shape=[jax.ShapeDtypeStruct((64, 128), f32)] * 4,
        cost_estimate=cost(256 * 128, 256 * 128 * 12),
        name="quarter",
    )(x_at, keep, came)


def gather_kernel(x_ref, q0, q1, q2, q3, out):
    for step, ref in enumerate((q0, q1, q2, q3)):
        at = pl.ds(pl.multiple_of(x_ref[step] * 64, 64), 64)
        out[at, :] = ref[...]


def gather(x_from, parts):
    return pl.pallas_call(
        gather_kernel,
        in_specs=[sm()] + [vm()] * 4,
        out_specs=vm(),
        out_shape=jax.ShapeDtypeStruct((256, 128), f32),
        cost_estimate=cost(0, 256 * 128 * 8),
        name="gather",
    )(x_from, *parts)


def root_kernel(core_ref, mine_ref, other_ref, prev_ref, stat_ref, root_ref, square_ref, packed, full):
    mine = pl.multiple_of(core_ref[0] * 256, 256)
    packed[pl.ds(mine, 256), :] = mine_ref[...]
    packed[pl.ds(256 - mine, 256), :] = other_ref[...]
    full[0:128, 0:128] = packed[0:128, :]
    full[0:128, 128:256] = packed[128:256, :]
    full[128:256, 0:128] = packed[128:256, :].T
    full[128:256, 128:256] = packed[256:384, :]
    full[256:288, 0:128] = packed[384:416, :]
    full[256:288, 128:256] = packed[416:448, :]
    full[256:288, 256:288] = packed[448:480, 0:32]
    strip = packed[384:448, :].T
    full[0:128, 256:288] = strip[:, 0:32]
    full[128:256, 256:288] = strip[:, 32:64]
    gram = full[...]
    statistic = stat_decay * prev_ref[...] + (1.0 - stat_decay) * gram
    stat_ref[...] = statistic
    norm = jnp.sqrt(jnp.sum(statistic * statistic, keepdims=True))
    row = lax.broadcasted_iota(jnp.int32, (BLOCK, BLOCK), 0)
    column = lax.broadcasted_iota(jnp.int32, (BLOCK, BLOCK), 1)
    five = jnp.where(row == column, f32(5.0), f32(0.0))
    normed = start_gain * statistic / norm
    factor = jnp.sqrt(jnp.sqrt(start_gain / norm))
    step = (five - normed) * 0.25
    step_pair = split(step)
    squared = split(dot3(step_pair, step_pair, MUL))
    fourth = split(dot3(squared, squared, MUL))
    second = (five - dot3(fourth, split(normed), MUL)) * 0.25
    root = dot3(step_pair, split(second), MUL) * factor
    root_ref[...] = root
    moved = dot3(split(gram), split(root), MUL)
    square_ref[...] = jnp.broadcast_to(jnp.sum(moved * root, keepdims=True), (8, 128))


def find_root(core, mine, other, prev):
    square = jax.ShapeDtypeStruct((BLOCK, BLOCK), f32)
    return pl.pallas_call(
        root_kernel,
        in_specs=[sm(), vm(), vm(), vm()],
        out_specs=[vm()] * 3,
        out_shape=[square, square, jax.ShapeDtypeStruct((8, 128), f32)],
        scratch_shapes=[pltpu.VMEM((512, 128), f32), pltpu.VMEM((BLOCK, BLOCK), f32)],
        compiler_params=params(32),
        cost_estimate=cost(36 * BLOCK**3, BLOCK * BLOCK * 16),
        name="root",
    )(core, mine, other, prev)


def move_kernel(root_ref, *refs):
    out = refs[-1]
    root = split(root_ref[...])
    place = 0
    for ref in refs[:-1]:
        rows = ref.shape[1]
        out[:, place : place + rows] = dot3(root, split(ref[...]), MUL)
        place += rows


def move(root, lives, rows):
    return pl.pallas_call(
        move_kernel,
        in_specs=[vm()] * (1 + len(lives)),
        out_specs=vm(),
        out_shape=jax.ShapeDtypeStruct((BLOCK, rows), f32),
        compiler_params=params(32),
        cost_estimate=cost(6 * BLOCK * BLOCK * rows, BLOCK * rows * 8),
        name="move",
    )(root, *lives)


def shards(grad_parts, embedding, stat_prev, row_flags):
    grad = grad_parts[0]
    shard_rows = grad.shape[0]
    dp = lax.axis_index("dp")
    vocab = lax.axis_index("vocab")
    y, z = dp // 4, dp % 4
    x, core = (vocab // 2) % 4, vocab % 2
    put = lambda value, pairs: lax.ppermute(value, "dp", pairs)
    vput = lambda value, pairs: lax.ppermute(value, "vocab", pairs)
    mask = (row_flags > 0).astype(f32)[None, :]
    y_at = [jnp.reshape((y + step) % 4, (1,)) for step in range(4)]
    z_at = jnp.stack([z ^ flip for flip in range(4)])
    x_to = jnp.stack([(x + step) % 4 for step in range(4)])
    x_from = jnp.stack([(x - step) % 4 for step in range(4)])
    core_at = jnp.reshape(core, (1,))

    lives, prior = [], None
    start = 0
    ties = []
    for number, rows in enumerate(SLICES):
        at = [y_at[step] for step in range(4)]
        if number >= 2:
            *at, token = lax.optimization_barrier((*at, ties[number - 2]))
        far = prep(grad, at[2], start, rows)
        right = prep(grad, at[1], start, rows)
        left = prep(grad, at[3], start, rows)
        own = prep(grad, at[0], start, rows)
        far_a, far_b = far
        right_a, right_b = right
        left_a, left_b = left
        if number >= 1:
            far_a, far_b, right_b, left_a, token = lax.optimization_barrier(
                (far_a, far_b, right_b, left_a, ties[number - 1])
            )
        came_up = put(far_a, y_move(1))
        came_down = put(far_b, y_move(-1))
        direct_up = put(right_b, y_move(1))
        direct_down = put(left_a, y_move(-1))
        ties.append(came_up[0, 0:8, 0:128] + came_down[0, 0:8, 0:128])
        sum_up = put(right_a + came_up, y_move(1))
        sum_down = put(left_b + came_down, y_move(-1))
        pieces = cut(z_at, (own[0], sum_up, direct_down, own[1], direct_up, sum_down), rows)
        whole = [pieces[0]] + [put(pieces[flip], z_flip(flip)) for flip in (1, 2, 3)]
        here = mask[:, start : start + rows]
        if number + 1 < len(SLICES):
            live, prior = finish(here, whole, prior, rows)
        else:
            live, keep, send = last(here, core_at, whole, prior, rows)
        lives.append(live)
        start += rows

    came = vput(send, v_move(0, 0, 1))
    quarters = quarter(x_to, keep, came)
    part = quarters[0]
    for step in (1, 2, 3):
        part = part + vput(quarters[step], v_move(0, step, 0))
    part = part + vput(part, v_move(1, 0, 0))
    parts = [part] + [vput(part, v_move(0, step, 0)) for step in (1, 2, 3)]
    mine = gather(x_from, parts)
    other = vput(mine, v_move(0, 0, 1))
    statistic, root, square = find_root(core_at, mine, other, stat_prev[0])

    total = square
    for step in (1, 2, 3):
        total = total + put(square, y_move(step))
    squares = total
    for flip in (1, 2, 3):
        squares = squares + put(total, z_flip(flip))
    direction = move(root, lives, shard_rows)
    entries = shard_rows * lax.axis_size("vocab") * BLOCK * lax.axis_size("dp")
    root_mean = jnp.sqrt(squares[0:1, 0:1] / entries + rms_epsilon)
    held = embedding.T
    stepped = (1.0 - learn_rate * weight_decay) * held - learn_rate * direction / root_mean
    updated = jnp.where(mask > 0, stepped, held).T
    panel = BLOCK // lax.axis_size("vocab")
    root_rows = lax.dynamic_slice_in_dim(root, vocab * panel, panel, 0)
    return (updated, statistic[None], root_rows[None])


def solution(mesh):
    placed = (P("dp", "vocab", None), P("vocab", "dp"), P("dp", None, None), P("vocab"))
    return jax.shard_map(
        shards,
        mesh=mesh,
        in_specs=placed,
        out_specs=(P("vocab", "dp"), P("dp", None, None), P("dp", "vocab", None)),
        check_vma=False,
    )
```

```python
import functools

import jax
import jax.numpy as jnp
from jax import lax
from jax.experimental import pallas as pl
from jax.experimental.pallas import tpu as pltpu
from jax.sharding import PartitionSpec as P

BLOCK = 288
HALF = 144
ROWS = 128
COUNT = 7
CUTS = ((4, 2), (6, 1))
LIMIT = 20

stat_decay = 0.8
learn_rate = 0.5
weight_decay = 0.1
rms_epsilon = 1e-06
start_gain = 2.5
f32 = jnp.float32
bf16 = jnp.bfloat16

ANY_T = (((1,), (1,)), ((), ()))
MUL = (((1,), (0,)), ((), ()))


def params(mib):
    return pltpu.CompilerParams(vmem_limit_bytes=mib * 2**20)


def cost(flops, moved):
    return pl.CostEstimate(flops=int(flops), bytes_accessed=int(moved), transcendentals=0)


def vm():
    return pl.BlockSpec(memory_space=pltpu.VMEM)


def hbm():
    return pl.BlockSpec(memory_space=pltpu.HBM)


def sm():
    return pl.BlockSpec(memory_space=pltpu.SMEM)


def y_move(step):
    return [(y * 4 + z, ((y + step) % 4) * 4 + z) for y in range(4) for z in range(4)]


def z_flip(mask):
    return [(y * 4 + z, y * 4 + (z ^ mask)) for y in range(4) for z in range(4)]


def v_move(dh, dx, dc):
    pairs = []
    for h in range(2):
        for x in range(4):
            for c in range(2):
                to = (((h + dh) % 2) * 4 + (x + dx) % 4) * 2 + (c + dc) % 2
                pairs.append(((h * 4 + x) * 2 + c, to))
    return pairs


def split(value):
    high = value.astype(bf16)
    low = (value - high.astype(f32)).astype(bf16)
    return high, low


def dot3(left, right, dims):
    (a, b), (c, d) = left, right
    one = lambda p, q: lax.dot_general(p, q, dims, preferred_element_type=f32)
    return one(a, c) + (one(a, d) + one(b, c))


def turn(grad_ref, held):
    for tile in range(9):
        place = tile * 128
        held[place : place + 128, :] = grad_ref[:, place : place + 128].astype(f32).T


def fetch(grad_ref, block, sem, number, column):
    column = pl.multiple_of(column * 1152, 128)
    rows = pl.ds(number * ROWS, ROWS)
    copy = pltpu.make_async_copy(grad_ref.at[rows, pl.ds(column, 1152)], block, sem)
    copy.start()
    return copy


def slots(step):
    return (2 if step < COUNT else 0) + (1 if 0 <= step - 2 < COUNT else 0)


PLAN = {1: ("side", 1), 3: ("side", 2), 5: (0, 1), 6: (0, 2), 7: (2, 1), 8: (2, 2)}


def blocks_of(step):
    count = 3 * (step < COUNT) + 2 * (0 <= step - 2 < COUNT)
    if step in PLAN:
        what, turned = PLAN[step]
        count += 4 if what == "side" else 2 * (turned == 1)
    return count


def halves(k):
    first = pl.ds(pl.multiple_of(k * BLOCK, 16), HALF)
    second = pl.ds(pl.multiple_of(k * BLOCK + HALF, 16), HALF)
    return first, second


def step_kernel(step, at_ref, grad_ref, *refs):
    refs = list(refs)
    held, blocks, sems = refs[-3:]
    count = 2 + (2 if step in PLAN and PLAN[step] != ("side", 1) else step in PLAN)
    given, (up, down, *outs) = refs[: -3 - count], refs[-3 - count : -3]
    copies = []

    def order(number, column):
        place = len(copies)
        copies.append(fetch(grad_ref, blocks.at[place], sems.at[place], number, column))

    if step < COUNT:
        order(step, at_ref[2])
        order(step, at_ref[1])
        order(step, at_ref[3])
    if 0 <= step - 2 < COUNT:
        order(step - 2, at_ref[1])
        order(step - 2, at_ref[3])
    what, turned = PLAN.get(step, (None, 0))
    if what == "side":
        for y in range(4):
            order(COUNT, y)
    elif turned == 1:
        for i in range(2):
            order(what + i, at_ref[0])
    taken = []

    def take():
        place = len(taken)
        copies[place].wait()
        taken.append(place)
        turn(blocks.at[place], held)

    whole = [k * BLOCK for k in range(4)]
    if step < COUNT:
        take()
        for k in range(4):
            up[0, k] = held[whole[k] : whole[k] + HALF, :]
            down[0, k] = held[whole[k] + HALF : whole[k] + BLOCK, :]
        take()
        for k in range(4):
            up[1, k] = held[whole[k] + HALF : whole[k] + BLOCK, :]
        take()
        for k in range(4):
            down[1, k] = held[whole[k] : whole[k] + HALF, :]
    if 0 <= step - 2 < COUNT:
        came_up, came_down = given[:2]
        given = given[2:]
        slot = slots(step) - 1
        take()
        for k in range(4):
            up[slot, k] = held[whole[k] : whole[k] + HALF, :] + came_up[0, k]
        take()
        for k in range(4):
            down[slot, k] = held[whole[k] + HALF : whole[k] + BLOCK, :] + came_down[0, k]
    if what == "side":
        for y in range(4):
            take()
            for place in range(2):
                k = at_ref[4 + (place * 2 + (turned == 1))]
                part = held[pl.ds(pl.multiple_of(k * BLOCK, 16), BLOCK), :]
                if turned == 1:
                    outs[0][place, y] = part
                else:
                    outs[place][y] = part + given[0][place, y]
    elif turned == 1:
        for i in range(2):
            take()
            direct_up, direct_down, sum_up, sum_down = given[4 * i : 4 * i + 4]
            slot = slots(what + i + 2) - 1
            lanes = slice(i * ROWS, (i + 1) * ROWS)
            for place in range(4):
                k = at_ref[4 + place]
                out = outs[1 - place % 2]
                first, second = halves(k)
                out[place // 2, 0:HALF, lanes] = held[first, :] + (sum_up[slot, k] + direct_down[1, k])
                out[place // 2, HALF:BLOCK, lanes] = held[second, :] + (sum_down[slot, k] + direct_up[1, k])
    elif turned == 2:
        for place in range(2):
            outs[place][...] = given[0][place] + given[1][place]


def scratch(count):
    return [
        pltpu.VMEM((1152, ROWS), f32),
        pltpu.VMEM((count, ROWS, 1152), bf16),
        pltpu.SemaphoreType.DMA((count,)),
    ]


def run_step(step, grad, where, came, crossing):
    given = list(came[step - 2]) if 0 <= step - 2 < COUNT else []
    shape = lambda *dims: jax.ShapeDtypeStruct(dims, f32)
    shapes = [shape(slots(step), 4, HALF, ROWS)] * 2
    what, turned = PLAN.get(step, (None, 0))
    if what == "side":
        shapes += [shape(2, 4, BLOCK, ROWS)] if turned == 1 else [shape(4, BLOCK, ROWS)] * 2
    elif turned == 1:
        for number in (what, what + 1):
            given += list(came[number]) + list(came[number + 2])
        shapes += [shape(2, BLOCK, 2 * ROWS)] * 2
    elif turned == 2:
        shapes += [shape(BLOCK, 2 * ROWS)] * 2
    if turned == 2:
        given += crossing
    return pl.pallas_call(
        functools.partial(step_kernel, step),
        in_specs=[sm(), hbm()] + [vm()] * len(given),
        out_specs=[vm()] * len(shapes),
        out_shape=shapes,
        scratch_shapes=scratch(blocks_of(step)),
        compiler_params=params(LIMIT),
        cost_estimate=cost(0, 22e6 * max(slots(step), 1)),
        name="step",
    )(where, grad, *given)


def cut_kernel(first, count, cross, at_ref, grad_ref, *refs):
    given, outs, (held, blocks, sems) = refs[: 4 * count], refs[4 * count : -3], refs[-3:]
    copies = [fetch(grad_ref, blocks.at[i], sems.at[i], first + i, at_ref[0]) for i in range(count)]
    for i in range(count):
        direct_up, direct_down, sum_up, sum_down = given[4 * i : 4 * i + 4]
        slot = slots(first + i + 2) - 1
        lanes = slice(i * ROWS, (i + 1) * ROWS)
        copies[i].wait()
        turn(blocks.at[i], held)
        for place in range(4):
            k, out, base = place, outs[0], place * BLOCK
            if cross:
                k, out, base = at_ref[4 + place], outs[place], 0
            first_half, second_half = halves(k)
            out[base : base + HALF, lanes] = held[first_half, :] + (sum_up[slot, k] + direct_down[1, k])
            out[base + HALF : base + BLOCK, lanes] = held[second_half, :] + (
                sum_down[slot, k] + direct_up[1, k]
            )


def cut(first, count, cross, grad, where, came):
    given = []
    for number in range(first, first + count):
        given += list(came[number]) + list(came[number + 2])
    rows = count * ROWS
    shapes = [jax.ShapeDtypeStruct((BLOCK, rows), f32)] * 4 if cross else [jax.ShapeDtypeStruct((1152, rows), f32)]
    return pl.pallas_call(
        functools.partial(cut_kernel, first, count, cross),
        in_specs=[sm(), hbm()] + [vm()] * len(given),
        out_specs=[vm()] * len(shapes),
        out_shape=shapes,
        scratch_shapes=scratch(count),
        compiler_params=params(LIMIT),
        cost_estimate=cost(0, rows * 1152 * 20),
        name="cut",
    )(where, grad, *given)


def side_cut_kernel(y_ref, kept, part, *outs):
    for step in range(4):
        outs[step][...] = kept[y_ref[step]] + part[y_ref[step]]


def side_cut(y_to, kept, part):
    return pl.pallas_call(
        side_cut_kernel,
        in_specs=[sm(), vm(), vm()],
        out_specs=[vm()] * 4,
        out_shape=[jax.ShapeDtypeStruct((BLOCK, ROWS), f32)] * 4,
        compiler_params=params(LIMIT),
        cost_estimate=cost(0, 1152 * ROWS * 8),
        name="side_cut",
    )(y_to, kept, part)


def pack(full, ref):
    ref[0:128, :] = full[0:128, 0:128]
    ref[128:256, :] = full[0:128, 128:256]
    ref[256:384, :] = full[128:256, 128:256]
    ref[384:416, :] = full[256:288, 0:128]
    ref[416:448, :] = full[256:288, 128:256]
    ref[448:480, 0:32] = full[256:288, 256:288]


def finish_kernel(count, mask_ref, *refs):
    parts, prior, (live_ref, gram_ref) = refs[:count], refs[count:-2], refs[-2:]
    live = sum_of(parts) * mask_ref[...]
    live_ref[...] = live
    pair = split(live)
    gram = dot3(pair, pair, ANY_T)
    gram_ref[...] = gram + prior[0][...] if prior else gram


def sum_of(refs):
    if len(refs) == 2:
        return refs[0][...] + refs[1][...]
    return (refs[0][...] + refs[1][...]) + (refs[2][...] + refs[3][...])


def finish(mask, parts, prior):
    prior = [] if prior is None else [prior]
    rows = parts[0].shape[1]
    return pl.pallas_call(
        functools.partial(finish_kernel, len(parts)),
        in_specs=[vm()] * (1 + len(parts) + len(prior)),
        out_specs=[vm()] * 2,
        out_shape=[
            jax.ShapeDtypeStruct((BLOCK, rows), f32),
            jax.ShapeDtypeStruct((BLOCK, BLOCK), f32),
        ],
        compiler_params=params(16),
        cost_estimate=cost(6 * BLOCK * BLOCK * rows, BLOCK * rows * 24),
        name="finish",
    )(mask, *parts, *prior)


def last_kernel(mask_ref, core_ref, p0, p1, p2, p3, prior, live_ref, keep_ref, send_ref, packed):
    live = ((p0[...] + p1[...]) + (p2[...] + p3[...])) * mask_ref[...]
    live_ref[...] = live
    pair = split(live)
    packed[...] = jnp.zeros_like(packed)
    pack(dot3(pair, pair, ANY_T) + prior[...], packed)
    mine = pl.multiple_of(core_ref[0] * 256, 256)
    keep_ref[...] = packed[pl.ds(mine, 256), :]
    send_ref[...] = packed[pl.ds(256 - mine, 256), :]


def last(mask, core, parts, prior, rows):
    return pl.pallas_call(
        last_kernel,
        in_specs=[vm(), sm()] + [vm()] * 5,
        out_specs=[vm()] * 3,
        out_shape=[
            jax.ShapeDtypeStruct((BLOCK, rows), f32),
            jax.ShapeDtypeStruct((256, 128), f32),
            jax.ShapeDtypeStruct((256, 128), f32),
        ],
        scratch_shapes=[pltpu.VMEM((512, 128), f32)],
        compiler_params=params(16),
        cost_estimate=cost(6 * BLOCK * BLOCK * rows, BLOCK * rows * 24),
        name="last",
    )(mask, core, *parts, prior)


def quarter_kernel(x_ref, keep, came, *outs):
    for step in range(4):
        at = pl.ds(pl.multiple_of(x_ref[step] * 64, 64), 64)
        outs[step][...] = keep[at, :] + came[at, :]


def quarter(x_at, keep, came):
    return pl.pallas_call(
        quarter_kernel,
        in_specs=[sm(), vm(), vm()],
        out_specs=[vm()] * 4,
        out_shape=[jax.ShapeDtypeStruct((64, 128), f32)] * 4,
        cost_estimate=cost(256 * 128, 256 * 128 * 12),
        compiler_params=params(8),
        name="quarter",
    )(x_at, keep, came)


def gather_kernel(x_ref, q0, q1, q2, q3, out):
    for step, ref in enumerate((q0, q1, q2, q3)):
        at = pl.ds(pl.multiple_of(x_ref[step] * 64, 64), 64)
        out[at, :] = ref[...]


def gather(x_from, parts):
    return pl.pallas_call(
        gather_kernel,
        in_specs=[sm()] + [vm()] * 4,
        out_specs=vm(),
        out_shape=jax.ShapeDtypeStruct((256, 128), f32),
        cost_estimate=cost(0, 256 * 128 * 8),
        compiler_params=params(8),
        name="gather",
    )(x_from, *parts)


def root_kernel(core_ref, mine_ref, other_ref, prev_ref, stat_ref, root_ref, square_ref, packed, full):
    mine = pl.multiple_of(core_ref[0] * 256, 256)
    packed[pl.ds(mine, 256), :] = mine_ref[...]
    packed[pl.ds(256 - mine, 256), :] = other_ref[...]
    full[0:128, 0:128] = packed[0:128, :]
    full[0:128, 128:256] = packed[128:256, :]
    full[128:256, 0:128] = packed[128:256, :].T
    full[128:256, 128:256] = packed[256:384, :]
    full[256:288, 0:128] = packed[384:416, :]
    full[256:288, 128:256] = packed[416:448, :]
    full[256:288, 256:288] = packed[448:480, 0:32]
    strip = packed[384:448, :].T
    full[0:128, 256:288] = strip[:, 0:32]
    full[128:256, 256:288] = strip[:, 32:64]
    gram = full[...]
    statistic = stat_decay * prev_ref[...] + (1.0 - stat_decay) * gram
    stat_ref[...] = statistic
    norm = jnp.sqrt(jnp.sum(statistic * statistic, keepdims=True))
    row = lax.broadcasted_iota(jnp.int32, (BLOCK, BLOCK), 0)
    column = lax.broadcasted_iota(jnp.int32, (BLOCK, BLOCK), 1)
    five = jnp.where(row == column, f32(5.0), f32(0.0))
    normed = start_gain * statistic / norm
    factor = jnp.sqrt(jnp.sqrt(start_gain / norm))
    step = (five - normed) * 0.25
    step_pair = split(step)
    squared = split(dot3(step_pair, step_pair, MUL))
    fourth = split(dot3(squared, squared, MUL))
    second = (five - dot3(fourth, split(normed), MUL)) * 0.25
    root = dot3(step_pair, split(second), MUL) * factor
    root_ref[...] = root
    moved = dot3(split(gram), split(root), MUL)
    square_ref[...] = jnp.broadcast_to(jnp.sum(moved * root, keepdims=True), (8, 128))


def find_root(core, mine, other, prev):
    square = jax.ShapeDtypeStruct((BLOCK, BLOCK), f32)
    return pl.pallas_call(
        root_kernel,
        in_specs=[sm(), vm(), vm(), vm()],
        out_specs=[vm()] * 3,
        out_shape=[square, square, jax.ShapeDtypeStruct((8, 128), f32)],
        scratch_shapes=[pltpu.VMEM((512, 128), f32), pltpu.VMEM((BLOCK, BLOCK), f32)],
        compiler_params=params(16),
        cost_estimate=cost(36 * BLOCK**3, BLOCK * BLOCK * 16),
        name="root",
    )(core, mine, other, prev)


def move_kernel(root_ref, *refs):
    out = refs[-1]
    root = split(root_ref[...])
    place = 0
    for ref in refs[:-1]:
        rows = ref.shape[1]
        out[:, place : place + rows] = dot3(root, split(ref[...]), MUL)
        place += rows


def move(root, lives, rows):
    return pl.pallas_call(
        move_kernel,
        in_specs=[vm()] * (1 + len(lives)),
        out_specs=vm(),
        out_shape=jax.ShapeDtypeStruct((BLOCK, rows), f32),
        compiler_params=params(16),
        cost_estimate=cost(6 * BLOCK * BLOCK * rows, BLOCK * rows * 8),
        name="move",
    )(root, *lives)


def shards(grad_parts, embedding, stat_prev, row_flags):
    grad = pltpu.with_memory_space_constraint(grad_parts[0], pltpu.HBM)
    shard_rows = grad.shape[0]
    dp = lax.axis_index("dp")
    vocab = lax.axis_index("vocab")
    y, z = dp // 4, dp % 4
    x, core = (vocab // 2) % 4, vocab % 2
    put = lambda value, pairs: lax.ppermute(value, "dp", pairs)
    vput = lambda value, pairs: lax.ppermute(value, "vocab", pairs)
    mask = (row_flags > 0).astype(f32)[None, :]
    y_at = [jnp.reshape((y + step) % 4, (1,)) for step in range(4)]
    z_at = jnp.stack([z ^ flip for flip in range(4)])
    x_to = jnp.stack([(x + step) % 4 for step in range(4)])
    x_from = jnp.stack([(x - step) % 4 for step in range(4)])
    core_at = jnp.reshape(core, (1,))

    y_to = jnp.concatenate(y_at)
    where = jnp.concatenate([y_to, z_at])
    came, crossed = {}, {}
    base, crossing = where, None
    for step in range(COUNT + 2):
        if step == 5:
            where, crossed["side"] = lax.optimization_barrier((where, crossed["side"]))
        elif step == 8:
            where, crossed[0] = lax.optimization_barrier((where, crossed[0]))
        outs = run_step(step, grad, where, came, crossing)
        where, outs = lax.optimization_barrier((where, outs))
        came[step] = (put(outs[0], y_move(1)), put(outs[1], y_move(-1)))
        what, turned = PLAN.get(step, (None, 0))
        if turned == 1:
            crossing = [*outs[3:], put(outs[2], z_flip(1))]
        elif turned == 2:
            crossed[what] = [outs[2], put(outs[3], z_flip(2))]
    y_last, where = lax.optimization_barrier((y_to, where))
    side_pieces = side_cut(y_last, *crossed.pop("side"))
    for first, count in CUTS:
        if first == 6:
            base, crossed[2] = lax.optimization_barrier((base, crossed[2]))
        pieces = cut(first, count, True, grad, base, came)
        crossed[first] = [pieces[0]] + [put(pieces[flip], z_flip(flip)) for flip in (1, 2, 3)]
    tail = [side_pieces[0]] + [put(side_pieces[turned], y_move(turned)) for turned in (1, 2, 3)]
    lives, prior = [], None
    place = 0
    for number in sorted(crossed):
        rows = crossed[number][0].shape[1]
        here = mask[:, place : place + rows]
        place += rows
        if number < 4:
            here, crossed[COUNT - 1][0] = lax.optimization_barrier((here, crossed[COUNT - 1][0]))
        if place < COUNT * ROWS:
            live, prior = finish(here, crossed[number], prior)
        else:
            side_live, prior = finish(mask[:, COUNT * ROWS :], tail, prior)
            live, keep, send = last(here, core_at, crossed[number], prior, ROWS)
        lives.append(live)
    lives.append(side_live)

    came = vput(send, v_move(0, 0, 1))
    quarters = quarter(x_to, keep, came)
    part = quarters[0]
    for step in (1, 2, 3):
        part = part + vput(quarters[step], v_move(0, step, 0))
    part = part + vput(part, v_move(1, 0, 0))
    parts = [part] + [vput(part, v_move(0, step, 0)) for step in (1, 2, 3)]
    mine = gather(x_from, parts)
    other = vput(mine, v_move(0, 0, 1))
    statistic, root, square = find_root(core_at, mine, other, stat_prev[0])

    total = square
    for step in (1, 2, 3):
        total = total + put(square, y_move(step))
    squares = total
    for flip in (1, 2, 3):
        squares = squares + put(total, z_flip(flip))
    direction = move(root, lives, shard_rows)
    entries = shard_rows * lax.axis_size("vocab") * BLOCK * lax.axis_size("dp")
    root_mean = jnp.sqrt(squares[0:1, 0:1] / entries + rms_epsilon)
    held = embedding.T
    stepped = (1.0 - learn_rate * weight_decay) * held - learn_rate * direction / root_mean
    updated = jnp.where(mask > 0, stepped, held).T
    panel = BLOCK // lax.axis_size("vocab")
    root_rows = lax.dynamic_slice_in_dim(root, vocab * panel, panel, 0)
    return (updated, statistic[None], root_rows[None])


def solution(mesh):
    placed = (P("dp", "vocab", None), P("vocab", "dp"), P("dp", None, None), P("vocab"))
    return jax.shard_map(
        shards,
        mesh=mesh,
        in_specs=placed,
        out_specs=(P("vocab", "dp"), P("dp", None, None), P("dp", "vocab", None)),
        check_vma=False,
    )
```

```python
import functools

import jax
import jax.numpy as jnp
from jax import lax
from jax.experimental import pallas as pl
from jax.experimental.pallas import tpu as pltpu
from jax.sharding import PartitionSpec as P

BLOCK = 288
HALF = 144
ROWS = 128
COUNT = 7
LIMIT = 20

stat_decay = 0.8
learn_rate = 0.5
weight_decay = 0.1
rms_epsilon = 1e-06
start_gain = 2.5
f32 = jnp.float32
bf16 = jnp.bfloat16

ANY_T = (((1,), (1,)), ((), ()))
MUL = (((1,), (0,)), ((), ()))


def params(mib):
    return pltpu.CompilerParams(vmem_limit_bytes=mib * 2**20)


def cost(flops, moved):
    return pl.CostEstimate(flops=int(flops), bytes_accessed=int(moved), transcendentals=0)


def vm():
    return pl.BlockSpec(memory_space=pltpu.VMEM)


def hbm():
    return pl.BlockSpec(memory_space=pltpu.HBM)


def sm():
    return pl.BlockSpec(memory_space=pltpu.SMEM)


def y_move(step):
    return [(y * 4 + z, ((y + step) % 4) * 4 + z) for y in range(4) for z in range(4)]


def z_flip(mask):
    return [(y * 4 + z, y * 4 + (z ^ mask)) for y in range(4) for z in range(4)]


def v_move(dh, dx, dc):
    pairs = []
    for h in range(2):
        for x in range(4):
            for c in range(2):
                to = (((h + dh) % 2) * 4 + (x + dx) % 4) * 2 + (c + dc) % 2
                pairs.append(((h * 4 + x) * 2 + c, to))
    return pairs


def split(value):
    high = value.astype(bf16)
    low = (value - high.astype(f32)).astype(bf16)
    return high, low


def dot3(left, right, dims):
    (a, b), (c, d) = left, right
    one = lambda p, q: lax.dot_general(p, q, dims, preferred_element_type=f32)
    return one(a, c) + (one(a, d) + one(b, c))


def turn(grad_ref, held):
    for tile in range(9):
        place = tile * 128
        held[place : place + 128, :] = grad_ref[:, place : place + 128].astype(f32).T


def fetch(grad_ref, block, sem, number, column):
    column = pl.multiple_of(column * 1152, 128)
    rows = pl.ds(number * ROWS, ROWS)
    copy = pltpu.make_async_copy(grad_ref.at[rows, pl.ds(column, 1152)], block, sem)
    copy.start()
    return copy


def slots(step):
    return (2 if step < COUNT else 0) + (1 if 0 <= step - 2 < COUNT else 0)


PLAN = {1: ("side", 1), 3: ("side", 2), 5: (0, 1), 6: (0, 2), 7: (2, 1), 8: (2, 2)}


def blocks_of(step):
    count = 3 * (step < COUNT) + 2 * (0 <= step - 2 < COUNT)
    if step in PLAN:
        what, turned = PLAN[step]
        count += 4 if what == "side" else 2 * (turned == 1)
    return count


def halves(k):
    first = pl.ds(pl.multiple_of(k * BLOCK, 16), HALF)
    second = pl.ds(pl.multiple_of(k * BLOCK + HALF, 16), HALF)
    return first, second


def step_kernel(step, at_ref, grad_ref, *refs):
    refs = list(refs)
    held, blocks, sems = refs[-3:]
    count = 2 + (2 if step in PLAN and PLAN[step] != ("side", 1) else step in PLAN)
    given, (up, down, *outs) = refs[: -3 - count], refs[-3 - count : -3]
    copies = []

    def order(number, column):
        place = len(copies)
        copies.append(fetch(grad_ref, blocks.at[place], sems.at[place], number, column))

    if step < COUNT:
        order(step, at_ref[2])
        order(step, at_ref[1])
        order(step, at_ref[3])
    if 0 <= step - 2 < COUNT:
        order(step - 2, at_ref[1])
        order(step - 2, at_ref[3])
    what, turned = PLAN.get(step, (None, 0))
    if what == "side":
        for y in range(4):
            order(COUNT, y)
    elif turned == 1:
        for i in range(2):
            order(what + i, at_ref[0])
    taken = []

    def take():
        place = len(taken)
        copies[place].wait()
        taken.append(place)
        turn(blocks.at[place], held)

    whole = [k * BLOCK for k in range(4)]
    if step < COUNT:
        take()
        for k in range(4):
            up[0, k] = held[whole[k] : whole[k] + HALF, :]
            down[0, k] = held[whole[k] + HALF : whole[k] + BLOCK, :]
        take()
        for k in range(4):
            up[1, k] = held[whole[k] + HALF : whole[k] + BLOCK, :]
        take()
        for k in range(4):
            down[1, k] = held[whole[k] : whole[k] + HALF, :]
    if 0 <= step - 2 < COUNT:
        came_up, came_down = given[:2]
        given = given[2:]
        slot = slots(step) - 1
        take()
        for k in range(4):
            up[slot, k] = held[whole[k] : whole[k] + HALF, :] + came_up[0, k]
        take()
        for k in range(4):
            down[slot, k] = held[whole[k] + HALF : whole[k] + BLOCK, :] + came_down[0, k]
    if what == "side":
        for y in range(4):
            take()
            for place in range(2):
                k = at_ref[4 + (place * 2 + (turned == 1))]
                part = held[pl.ds(pl.multiple_of(k * BLOCK, 16), BLOCK), :]
                if turned == 1:
                    outs[0][place, y] = part
                else:
                    outs[place][y] = part + given[0][place, y]
    elif turned == 1:
        for i in range(2):
            take()
            lanes = slice(i * ROWS, (i + 1) * ROWS)
            share(at_ref, held, given[4 * i : 4 * i + 4], slots(what + i + 2) - 1, outs[0], outs[1], lanes)
    elif turned == 2:
        for place in range(2):
            outs[place][...] = given[0][place] + given[1][place]


def scratch(count):
    return [
        pltpu.VMEM((1152, ROWS), f32),
        pltpu.VMEM((count, ROWS, 1152), bf16),
        pltpu.SemaphoreType.DMA((count,)),
    ]


def run_step(step, grad, where, came, crossing):
    given = list(came[step - 2]) if 0 <= step - 2 < COUNT else []
    shape = lambda *dims: jax.ShapeDtypeStruct(dims, f32)
    shapes = [shape(slots(step), 4, HALF, ROWS)] * 2
    what, turned = PLAN.get(step, (None, 0))
    if what == "side":
        shapes += [shape(2, 4, BLOCK, ROWS)] if turned == 1 else [shape(4, BLOCK, ROWS)] * 2
    elif turned == 1:
        for number in (what, what + 1):
            given += list(came[number]) + list(came[number + 2])
        shapes += [shape(2, BLOCK, 2 * ROWS)] * 2
    elif turned == 2:
        shapes += [shape(BLOCK, 2 * ROWS)] * 2
    if turned == 2:
        given += crossing
    return pl.pallas_call(
        functools.partial(step_kernel, step),
        in_specs=[sm(), hbm()] + [vm()] * len(given),
        out_specs=[vm()] * len(shapes),
        out_shape=shapes,
        scratch_shapes=scratch(blocks_of(step)),
        compiler_params=params(LIMIT),
        cost_estimate=cost(0, 22e6 * max(slots(step), 1)),
        name="step",
    )(where, grad, *given)


def share(at_ref, held, came, slot, leaves, stays, lanes):
    direct_up, direct_down, sum_up, sum_down = came
    for place in range(4):
        k = at_ref[4 + place]
        out = (stays, leaves)[place % 2]
        first, second = halves(k)
        out[place // 2, 0:HALF, lanes] = held[first, :] + (sum_up[slot, k] + direct_down[1, k])
        out[place // 2, HALF:BLOCK, lanes] = held[second, :] + (sum_down[slot, k] + direct_up[1, k])


def cut_kernel(number, at_ref, grad_ref, *refs):
    came, (leaves, stays, held, blocks, sems) = refs[:4], refs[4:]
    copy = fetch(grad_ref, blocks.at[0], sems.at[0], number, at_ref[0])
    copy.wait()
    turn(blocks.at[0], held)
    share(at_ref, held, came, slots(number + 2) - 1, leaves, stays, slice(0, ROWS))


def cut(number, grad, where, came):
    return pl.pallas_call(
        functools.partial(cut_kernel, number),
        in_specs=[sm(), hbm()] + [vm()] * 4,
        out_specs=[vm()] * 2,
        out_shape=[jax.ShapeDtypeStruct((2, BLOCK, ROWS), f32)] * 2,
        scratch_shapes=scratch(1),
        compiler_params=params(LIMIT),
        cost_estimate=cost(0, ROWS * 1152 * 20),
        name="cut",
    )(where, grad, *came[number], *came[number + 2])


def mix_kernel(stays, came, kept, leaves):
    kept[...] = stays[0] + came[0]
    leaves[...] = stays[1] + came[1]


def mix(stays, came):
    return pl.pallas_call(
        mix_kernel,
        in_specs=[vm()] * 2,
        out_specs=[vm()] * 2,
        out_shape=[jax.ShapeDtypeStruct((BLOCK, ROWS), f32)] * 2,
        compiler_params=params(LIMIT),
        cost_estimate=cost(0, ROWS * 1152 * 6),
        name="mix",
    )(stays, came)


def side_cut_kernel(y_ref, kept, part, *outs):
    for step in range(4):
        outs[step][...] = kept[y_ref[step]] + part[y_ref[step]]


def side_cut(y_to, kept, part):
    return pl.pallas_call(
        side_cut_kernel,
        in_specs=[sm(), vm(), vm()],
        out_specs=[vm()] * 4,
        out_shape=[jax.ShapeDtypeStruct((BLOCK, ROWS), f32)] * 4,
        compiler_params=params(LIMIT),
        cost_estimate=cost(0, 1152 * ROWS * 8),
        name="side_cut",
    )(y_to, kept, part)


def pack(full, ref):
    ref[0:128, :] = full[0:128, 0:128]
    ref[128:256, :] = full[0:128, 128:256]
    ref[256:384, :] = full[128:256, 128:256]
    ref[384:416, :] = full[256:288, 0:128]
    ref[416:448, :] = full[256:288, 128:256]
    ref[448:480, 0:32] = full[256:288, 256:288]


def finish_kernel(count, mask_ref, *refs):
    parts, prior, (live_ref, gram_ref) = refs[:count], refs[count:-2], refs[-2:]
    live = sum_of(parts) * mask_ref[...]
    live_ref[...] = live
    pair = split(live)
    gram = dot3(pair, pair, ANY_T)
    gram_ref[...] = gram + prior[0][...] if prior else gram


def sum_of(refs):
    if len(refs) == 2:
        return refs[0][...] + refs[1][...]
    return (refs[0][...] + refs[1][...]) + (refs[2][...] + refs[3][...])


def finish(mask, parts, prior):
    prior = [] if prior is None else [prior]
    rows = parts[0].shape[1]
    return pl.pallas_call(
        functools.partial(finish_kernel, len(parts)),
        in_specs=[vm()] * (1 + len(parts) + len(prior)),
        out_specs=[vm()] * 2,
        out_shape=[
            jax.ShapeDtypeStruct((BLOCK, rows), f32),
            jax.ShapeDtypeStruct((BLOCK, BLOCK), f32),
        ],
        compiler_params=params(16),
        cost_estimate=cost(6 * BLOCK * BLOCK * rows, BLOCK * rows * 24),
        name="finish",
    )(mask, *parts, *prior)


def last_kernel(mask_ref, core_ref, p0, p1, prior, live_ref, keep_ref, send_ref, packed):
    live = (p0[...] + p1[...]) * mask_ref[...]
    live_ref[...] = live
    pair = split(live)
    packed[...] = jnp.zeros_like(packed)
    pack(dot3(pair, pair, ANY_T) + prior[...], packed)
    mine = pl.multiple_of(core_ref[0] * 256, 256)
    keep_ref[...] = packed[pl.ds(mine, 256), :]
    send_ref[...] = packed[pl.ds(256 - mine, 256), :]


def last(mask, core, parts, prior, rows):
    return pl.pallas_call(
        last_kernel,
        in_specs=[vm(), sm()] + [vm()] * 3,
        out_specs=[vm()] * 3,
        out_shape=[
            jax.ShapeDtypeStruct((BLOCK, rows), f32),
            jax.ShapeDtypeStruct((256, 128), f32),
            jax.ShapeDtypeStruct((256, 128), f32),
        ],
        scratch_shapes=[pltpu.VMEM((512, 128), f32)],
        compiler_params=params(16),
        cost_estimate=cost(6 * BLOCK * BLOCK * rows, BLOCK * rows * 24),
        name="last",
    )(mask, core, *parts, prior)


def quarter_kernel(x_ref, keep, came, *outs):
    for step in range(4):
        at = pl.ds(pl.multiple_of(x_ref[step] * 64, 64), 64)
        outs[step][...] = keep[at, :] + came[at, :]


def quarter(x_at, keep, came):
    return pl.pallas_call(
        quarter_kernel,
        in_specs=[sm(), vm(), vm()],
        out_specs=[vm()] * 4,
        out_shape=[jax.ShapeDtypeStruct((64, 128), f32)] * 4,
        cost_estimate=cost(256 * 128, 256 * 128 * 12),
        compiler_params=params(8),
        name="quarter",
    )(x_at, keep, came)


def gather_kernel(x_ref, q0, q1, q2, q3, out):
    for step, ref in enumerate((q0, q1, q2, q3)):
        at = pl.ds(pl.multiple_of(x_ref[step] * 64, 64), 64)
        out[at, :] = ref[...]


def gather(x_from, parts):
    return pl.pallas_call(
        gather_kernel,
        in_specs=[sm()] + [vm()] * 4,
        out_specs=vm(),
        out_shape=jax.ShapeDtypeStruct((256, 128), f32),
        cost_estimate=cost(0, 256 * 128 * 8),
        compiler_params=params(8),
        name="gather",
    )(x_from, *parts)


def root_kernel(core_ref, mine_ref, other_ref, prev_ref, stat_ref, root_ref, square_ref, packed, full):
    mine = pl.multiple_of(core_ref[0] * 256, 256)
    packed[pl.ds(mine, 256), :] = mine_ref[...]
    packed[pl.ds(256 - mine, 256), :] = other_ref[...]
    full[0:128, 0:128] = packed[0:128, :]
    full[0:128, 128:256] = packed[128:256, :]
    full[128:256, 0:128] = packed[128:256, :].T
    full[128:256, 128:256] = packed[256:384, :]
    full[256:288, 0:128] = packed[384:416, :]
    full[256:288, 128:256] = packed[416:448, :]
    full[256:288, 256:288] = packed[448:480, 0:32]
    strip = packed[384:448, :].T
    full[0:128, 256:288] = strip[:, 0:32]
    full[128:256, 256:288] = strip[:, 32:64]
    gram = full[...]
    statistic = stat_decay * prev_ref[...] + (1.0 - stat_decay) * gram
    stat_ref[...] = statistic
    norm = jnp.sqrt(jnp.sum(statistic * statistic, keepdims=True))
    row = lax.broadcasted_iota(jnp.int32, (BLOCK, BLOCK), 0)
    column = lax.broadcasted_iota(jnp.int32, (BLOCK, BLOCK), 1)
    five = jnp.where(row == column, f32(5.0), f32(0.0))
    normed = start_gain * statistic / norm
    factor = jnp.sqrt(jnp.sqrt(start_gain / norm))
    step = (five - normed) * 0.25
    step_pair = split(step)
    squared = split(dot3(step_pair, step_pair, MUL))
    fourth = split(dot3(squared, squared, MUL))
    second = (five - dot3(fourth, split(normed), MUL)) * 0.25
    root = dot3(step_pair, split(second), MUL) * factor
    root_ref[...] = root
    moved = dot3(split(gram), split(root), MUL)
    square_ref[...] = jnp.broadcast_to(jnp.sum(moved * root, keepdims=True), (8, 128))


def find_root(core, mine, other, prev):
    square = jax.ShapeDtypeStruct((BLOCK, BLOCK), f32)
    return pl.pallas_call(
        root_kernel,
        in_specs=[sm(), vm(), vm(), vm()],
        out_specs=[vm()] * 3,
        out_shape=[square, square, jax.ShapeDtypeStruct((8, 128), f32)],
        scratch_shapes=[pltpu.VMEM((512, 128), f32), pltpu.VMEM((BLOCK, BLOCK), f32)],
        compiler_params=params(16),
        cost_estimate=cost(36 * BLOCK**3, BLOCK * BLOCK * 16),
        name="root",
    )(core, mine, other, prev)


def move_kernel(root_ref, *refs):
    out = refs[-1]
    root = split(root_ref[...])
    place = 0
    for ref in refs[:-1]:
        rows = ref.shape[1]
        out[:, place : place + rows] = dot3(root, split(ref[...]), MUL)
        place += rows


def move(root, lives, rows):
    return pl.pallas_call(
        move_kernel,
        in_specs=[vm()] * (1 + len(lives)),
        out_specs=vm(),
        out_shape=jax.ShapeDtypeStruct((BLOCK, rows), f32),
        compiler_params=params(16),
        cost_estimate=cost(6 * BLOCK * BLOCK * rows, BLOCK * rows * 8),
        name="move",
    )(root, *lives)


def shards(grad_parts, embedding, stat_prev, row_flags):
    grad = pltpu.with_memory_space_constraint(grad_parts[0], pltpu.HBM)
    shard_rows = grad.shape[0]
    dp = lax.axis_index("dp")
    vocab = lax.axis_index("vocab")
    y, z = dp // 4, dp % 4
    x, core = (vocab // 2) % 4, vocab % 2
    put = lambda value, pairs: lax.ppermute(value, "dp", pairs)
    vput = lambda value, pairs: lax.ppermute(value, "vocab", pairs)
    mask = (row_flags > 0).astype(f32)[None, :]
    y_at = [jnp.reshape((y + step) % 4, (1,)) for step in range(4)]
    z_at = jnp.stack([z ^ flip for flip in range(4)])
    x_to = jnp.stack([(x + step) % 4 for step in range(4)])
    x_from = jnp.stack([(x - step) % 4 for step in range(4)])
    core_at = jnp.reshape(core, (1,))

    y_to = jnp.concatenate(y_at)
    where = jnp.concatenate([y_to, z_at])
    came, crossed = {}, {}
    base, crossing = where, None
    for step in range(COUNT + 2):
        if step == 5:
            where, crossed["side"] = lax.optimization_barrier((where, crossed["side"]))
        elif step == 7:
            where, crossed[0] = lax.optimization_barrier((where, crossed[0]))
        outs = run_step(step, grad, where, came, crossing)
        where, outs = lax.optimization_barrier((where, outs))
        came[step] = (put(outs[0], y_move(1)), put(outs[1], y_move(-1)))
        what, turned = PLAN.get(step, (None, 0))
        if turned == 1:
            crossing = [*outs[3:], put(outs[2], z_flip(1))]
        elif turned == 2:
            crossed[what] = [outs[2], put(outs[3], z_flip(2))]
    sent, first = {}, {}
    for number in (4, 5, 6):
        if number == 6:
            where, crossed[2], first[4] = lax.optimization_barrier((where, crossed[2], first[4]))
        sent[number] = cut(number, grad, where, came)
        first[number] = put(sent[number][0], z_flip(1))
    y_last, sent[6] = lax.optimization_barrier((y_to, sent[6]))
    side_pieces = side_cut(y_last, *crossed.pop("side"))
    tail = [side_pieces[0]] + [put(side_pieces[turned], y_move(turned)) for turned in (1, 2, 3)]
    for number in (4, 5, 6):
        if number == 6:
            first[6], crossed[4] = lax.optimization_barrier((first[6], crossed[4]))
        kept, leaves = mix(sent[number][1], first[number])
        crossed[number] = [kept, put(leaves, z_flip(2))]
    lives, prior = [], None
    place = 0
    for number in sorted(crossed):
        rows = crossed[number][0].shape[1]
        here = mask[:, place : place + rows]
        place += rows
        if number < 4:
            here, crossed[COUNT - 1][0] = lax.optimization_barrier((here, crossed[COUNT - 1][0]))
        if place < COUNT * ROWS:
            live, prior = finish(here, crossed[number], prior)
        else:
            side_live, prior = finish(mask[:, COUNT * ROWS :], tail, prior)
            live, keep, send = last(here, core_at, crossed[number], prior, ROWS)
        lives.append(live)
    lives.append(side_live)

    came = vput(send, v_move(0, 0, 1))
    quarters = quarter(x_to, keep, came)
    part = quarters[0]
    for step in (1, 2, 3):
        part = part + vput(quarters[step], v_move(0, step, 0))
    part = part + vput(part, v_move(1, 0, 0))
    parts = [part] + [vput(part, v_move(0, step, 0)) for step in (1, 2, 3)]
    mine = gather(x_from, parts)
    other = vput(mine, v_move(0, 0, 1))
    statistic, root, square = find_root(core_at, mine, other, stat_prev[0])

    total = square
    for step in (1, 2, 3):
        total = total + put(square, y_move(step))
    squares = total
    for flip in (1, 2, 3):
        squares = squares + put(total, z_flip(flip))
    direction = move(root, lives, shard_rows)
    entries = shard_rows * lax.axis_size("vocab") * BLOCK * lax.axis_size("dp")
    root_mean = jnp.sqrt(squares[0:1, 0:1] / entries + rms_epsilon)
    held = embedding.T
    stepped = (1.0 - learn_rate * weight_decay) * held - learn_rate * direction / root_mean
    updated = jnp.where(mask > 0, stepped, held).T
    panel = BLOCK // lax.axis_size("vocab")
    root_rows = lax.dynamic_slice_in_dim(root, vocab * panel, panel, 0)
    return (updated, statistic[None], root_rows[None])


def solution(mesh):
    placed = (P("dp", "vocab", None), P("vocab", "dp"), P("dp", None, None), P("vocab"))
    return jax.shard_map(
        shards,
        mesh=mesh,
        in_specs=placed,
        out_specs=(P("vocab", "dp"), P("dp", None, None), P("dp", "vocab", None)),
        check_vma=False,
    )
```

```python
import functools

import jax
import jax.numpy as jnp
from jax import lax
from jax.experimental import pallas as pl
from jax.experimental.pallas import tpu as pltpu
from jax.sharding import PartitionSpec as P

BLOCK = 288
HALF = 144
ROWS = 128
COUNT = 7
LIMIT = 20

stat_decay = 0.8
learn_rate = 0.5
weight_decay = 0.1
rms_epsilon = 1e-06
start_gain = 2.5
f32 = jnp.float32
bf16 = jnp.bfloat16

ANY_T = (((1,), (1,)), ((), ()))
MUL = (((1,), (0,)), ((), ()))


def params(mib):
    return pltpu.CompilerParams(vmem_limit_bytes=mib * 2**20)


def cost(flops, moved):
    return pl.CostEstimate(flops=int(flops), bytes_accessed=int(moved), transcendentals=0)


def vm():
    return pl.BlockSpec(memory_space=pltpu.VMEM)


def hbm():
    return pl.BlockSpec(memory_space=pltpu.HBM)


def sm():
    return pl.BlockSpec(memory_space=pltpu.SMEM)


def y_move(step):
    return [(y * 4 + z, ((y + step) % 4) * 4 + z) for y in range(4) for z in range(4)]


def z_flip(mask):
    return [(y * 4 + z, y * 4 + (z ^ mask)) for y in range(4) for z in range(4)]


def v_move(dh, dx, dc):
    pairs = []
    for h in range(2):
        for x in range(4):
            for c in range(2):
                to = (((h + dh) % 2) * 4 + (x + dx) % 4) * 2 + (c + dc) % 2
                pairs.append(((h * 4 + x) * 2 + c, to))
    return pairs


def split(value):
    high = value.astype(bf16)
    low = (value - high.astype(f32)).astype(bf16)
    return high, low


def dot3(left, right, dims):
    (a, b), (c, d) = left, right
    one = lambda p, q: lax.dot_general(p, q, dims, preferred_element_type=f32)
    return one(a, c) + (one(a, d) + one(b, c))


def turn(grad_ref, held):
    for tile in range(9):
        place = tile * 128
        held[place : place + 128, :] = grad_ref[:, place : place + 128].astype(f32).T


def fetch(grad_ref, block, sem, number, column):
    column = pl.multiple_of(column * 1152, 128)
    rows = pl.ds(number * ROWS, ROWS)
    copy = pltpu.make_async_copy(grad_ref.at[rows, pl.ds(column, 1152)], block, sem)
    copy.start()
    return copy


def slots(step):
    return (2 if step < COUNT else 0) + (1 if 0 <= step - 2 < COUNT else 0)


PLAN = {0: ("side", 1), 3: ("side", 2), 5: (0, 1), 6: (0, 2), 7: (2, 1), 8: (2, 2)}


def blocks_of(step):
    count = 3 * (step < COUNT) + 2 * (0 <= step - 2 < COUNT)
    if step in PLAN:
        what, turned = PLAN[step]
        count += 4 if what == "side" else 2 * (turned == 1)
    return count


def halves(k):
    first = pl.ds(pl.multiple_of(k * BLOCK, 16), HALF)
    second = pl.ds(pl.multiple_of(k * BLOCK + HALF, 16), HALF)
    return first, second


def step_kernel(step, at_ref, grad_ref, *refs):
    refs = list(refs)
    held, blocks, sems = refs[-3:]
    count = 2 + (2 if step in PLAN and PLAN[step] != ("side", 1) else step in PLAN)
    given, (up, down, *outs) = refs[: -3 - count], refs[-3 - count : -3]
    copies = []

    def order(number, column):
        place = len(copies)
        copies.append(fetch(grad_ref, blocks.at[place], sems.at[place], number, column))

    if step < COUNT:
        order(step, at_ref[2])
        order(step, at_ref[1])
        order(step, at_ref[3])
    if 0 <= step - 2 < COUNT:
        order(step - 2, at_ref[1])
        order(step - 2, at_ref[3])
    what, turned = PLAN.get(step, (None, 0))
    if what == "side":
        for y in range(4):
            order(COUNT, y)
    elif turned == 1:
        for i in range(2):
            order(what + i, at_ref[0])
    taken = []

    def take():
        place = len(taken)
        copies[place].wait()
        taken.append(place)
        turn(blocks.at[place], held)

    whole = [k * BLOCK for k in range(4)]
    if step < COUNT:
        take()
        for k in range(4):
            up[0, k] = held[whole[k] : whole[k] + HALF, :]
            down[0, k] = held[whole[k] + HALF : whole[k] + BLOCK, :]
        take()
        for k in range(4):
            up[1, k] = held[whole[k] + HALF : whole[k] + BLOCK, :]
        take()
        for k in range(4):
            down[1, k] = held[whole[k] : whole[k] + HALF, :]
    if 0 <= step - 2 < COUNT:
        came_up, came_down = given[:2]
        given = given[2:]
        slot = slots(step) - 1
        take()
        for k in range(4):
            up[slot, k] = held[whole[k] : whole[k] + HALF, :] + came_up[0, k]
        take()
        for k in range(4):
            down[slot, k] = held[whole[k] + HALF : whole[k] + BLOCK, :] + came_down[0, k]
    if what == "side":
        for y in range(4):
            take()
            for place in range(2):
                k = at_ref[4 + (place * 2 + (turned == 1))]
                part = held[pl.ds(pl.multiple_of(k * BLOCK, 16), BLOCK), :]
                if turned == 1:
                    outs[0][place, y] = part
                else:
                    outs[place][y] = part + given[0][place, y]
    elif turned == 1:
        for i in range(2):
            take()
            lanes = slice(i * ROWS, (i + 1) * ROWS)
            share(at_ref, held, given[4 * i : 4 * i + 4], slots(what + i + 2) - 1, outs[0], outs[1], lanes)
    elif turned == 2:
        for place in range(2):
            outs[place][...] = given[0][place] + given[1][place]


def scratch(count):
    return [
        pltpu.VMEM((1152, ROWS), f32),
        pltpu.VMEM((count, ROWS, 1152), bf16),
        pltpu.SemaphoreType.DMA((count,)),
    ]


def run_step(step, grad, where, came, crossing):
    given = list(came[step - 2]) if 0 <= step - 2 < COUNT else []
    shape = lambda *dims: jax.ShapeDtypeStruct(dims, f32)
    shapes = [shape(slots(step), 4, HALF, ROWS)] * 2
    what, turned = PLAN.get(step, (None, 0))
    if what == "side":
        shapes += [shape(2, 4, BLOCK, ROWS)] if turned == 1 else [shape(4, BLOCK, ROWS)] * 2
    elif turned == 1:
        for number in (what, what + 1):
            given += list(came[number]) + list(came[number + 2])
        shapes += [shape(2, BLOCK, 2 * ROWS)] * 2
    elif turned == 2:
        shapes += [shape(BLOCK, 2 * ROWS)] * 2
    if turned == 2:
        given += crossing
    return pl.pallas_call(
        functools.partial(step_kernel, step),
        in_specs=[sm(), hbm()] + [vm()] * len(given),
        out_specs=[vm()] * len(shapes),
        out_shape=shapes,
        scratch_shapes=scratch(blocks_of(step)),
        compiler_params=params(LIMIT),
        cost_estimate=cost(0, 22e6 * max(slots(step), 1)),
        name="step",
    )(where, grad, *given)


def share(at_ref, held, came, slot, leaves, stays, lanes):
    direct_up, direct_down, sum_up, sum_down = came
    for place in range(4):
        k = at_ref[4 + place]
        out = (stays, leaves)[place % 2]
        first, second = halves(k)
        out[place // 2, 0:HALF, lanes] = held[first, :] + (sum_up[slot, k] + direct_down[1, k])
        out[place // 2, HALF:BLOCK, lanes] = held[second, :] + (sum_down[slot, k] + direct_up[1, k])


def cut_kernel(number, at_ref, grad_ref, *refs):
    came, (leaves, stays, held, blocks, sems) = refs[:4], refs[4:]
    copy = fetch(grad_ref, blocks.at[0], sems.at[0], number, at_ref[0])
    copy.wait()
    turn(blocks.at[0], held)
    share(at_ref, held, came, slots(number + 2) - 1, leaves, stays, slice(0, ROWS))


def cut(number, grad, where, came):
    return pl.pallas_call(
        functools.partial(cut_kernel, number),
        in_specs=[sm(), hbm()] + [vm()] * 4,
        out_specs=[vm()] * 2,
        out_shape=[jax.ShapeDtypeStruct((2, BLOCK, ROWS), f32)] * 2,
        scratch_shapes=scratch(1),
        compiler_params=params(LIMIT),
        cost_estimate=cost(0, ROWS * 1152 * 20),
        name="cut",
    )(where, grad, *came[number], *came[number + 2])


def mix_kernel(stays, came, kept, leaves):
    kept[...] = stays[0] + came[0]
    leaves[...] = stays[1] + came[1]


def mix(stays, came):
    return pl.pallas_call(
        mix_kernel,
        in_specs=[vm()] * 2,
        out_specs=[vm()] * 2,
        out_shape=[jax.ShapeDtypeStruct((BLOCK, ROWS), f32)] * 2,
        compiler_params=params(LIMIT),
        cost_estimate=cost(0, ROWS * 1152 * 6),
        name="mix",
    )(stays, came)


def side_cut_kernel(y_ref, kept, part, *outs):
    for step in range(4):
        outs[step][...] = kept[y_ref[step]] + part[y_ref[step]]


def side_cut(y_to, kept, part):
    return pl.pallas_call(
        side_cut_kernel,
        in_specs=[sm(), vm(), vm()],
        out_specs=[vm()] * 4,
        out_shape=[jax.ShapeDtypeStruct((BLOCK, ROWS), f32)] * 4,
        compiler_params=params(LIMIT),
        cost_estimate=cost(0, 1152 * ROWS * 8),
        name="side_cut",
    )(y_to, kept, part)


def pack(full, ref):
    ref[0:128, :] = full[0:128, 0:128]
    ref[128:256, :] = full[0:128, 128:256]
    ref[256:384, :] = full[128:256, 128:256]
    ref[384:416, :] = full[256:288, 0:128]
    ref[416:448, :] = full[256:288, 128:256]
    ref[448:480, 0:32] = full[256:288, 256:288]


def finish_kernel(count, mask_ref, *refs):
    parts, prior, (live_ref, gram_ref) = refs[:count], refs[count:-2], refs[-2:]
    live = sum_of(parts) * mask_ref[...]
    live_ref[...] = live
    pair = split(live)
    gram = dot3(pair, pair, ANY_T)
    gram_ref[...] = gram + prior[0][...] if prior else gram


def sum_of(refs):
    if len(refs) == 2:
        return refs[0][...] + refs[1][...]
    return (refs[0][...] + refs[1][...]) + (refs[2][...] + refs[3][...])


def finish(mask, parts, prior):
    prior = [] if prior is None else [prior]
    rows = parts[0].shape[1]
    return pl.pallas_call(
        functools.partial(finish_kernel, len(parts)),
        in_specs=[vm()] * (1 + len(parts) + len(prior)),
        out_specs=[vm()] * 2,
        out_shape=[
            jax.ShapeDtypeStruct((BLOCK, rows), f32),
            jax.ShapeDtypeStruct((BLOCK, BLOCK), f32),
        ],
        compiler_params=params(16),
        cost_estimate=cost(6 * BLOCK * BLOCK * rows, BLOCK * rows * 24),
        name="finish",
    )(mask, *parts, *prior)


def last_kernel(mask_ref, core_ref, p0, p1, prior, live_ref, keep_ref, send_ref, packed):
    live = (p0[...] + p1[...]) * mask_ref[...]
    live_ref[...] = live
    pair = split(live)
    packed[...] = jnp.zeros_like(packed)
    pack(dot3(pair, pair, ANY_T) + prior[...], packed)
    mine = pl.multiple_of(core_ref[0] * 256, 256)
    keep_ref[...] = packed[pl.ds(mine, 256), :]
    send_ref[...] = packed[pl.ds(256 - mine, 256), :]


def last(mask, core, parts, prior, rows):
    return pl.pallas_call(
        last_kernel,
        in_specs=[vm(), sm()] + [vm()] * 3,
        out_specs=[vm()] * 3,
        out_shape=[
            jax.ShapeDtypeStruct((BLOCK, rows), f32),
            jax.ShapeDtypeStruct((256, 128), f32),
            jax.ShapeDtypeStruct((256, 128), f32),
        ],
        scratch_shapes=[pltpu.VMEM((512, 128), f32)],
        compiler_params=params(16),
        cost_estimate=cost(6 * BLOCK * BLOCK * rows, BLOCK * rows * 24),
        name="last",
    )(mask, core, *parts, prior)


def quarter_kernel(x_ref, keep, came, *outs):
    for step in range(4):
        at = pl.ds(pl.multiple_of(x_ref[step] * 64, 64), 64)
        outs[step][...] = keep[at, :] + came[at, :]


def quarter(x_at, keep, came):
    return pl.pallas_call(
        quarter_kernel,
        in_specs=[sm(), vm(), vm()],
        out_specs=[vm()] * 4,
        out_shape=[jax.ShapeDtypeStruct((64, 128), f32)] * 4,
        cost_estimate=cost(256 * 128, 256 * 128 * 12),
        compiler_params=params(8),
        name="quarter",
    )(x_at, keep, came)


def gather_kernel(x_ref, q0, q1, q2, q3, out):
    for step, ref in enumerate((q0, q1, q2, q3)):
        at = pl.ds(pl.multiple_of(x_ref[step] * 64, 64), 64)
        out[at, :] = ref[...]


def gather(x_from, parts):
    return pl.pallas_call(
        gather_kernel,
        in_specs=[sm()] + [vm()] * 4,
        out_specs=vm(),
        out_shape=jax.ShapeDtypeStruct((256, 128), f32),
        cost_estimate=cost(0, 256 * 128 * 8),
        compiler_params=params(8),
        name="gather",
    )(x_from, *parts)


def root_kernel(core_ref, mine_ref, other_ref, prev_ref, stat_ref, root_ref, square_ref, packed, full):
    mine = pl.multiple_of(core_ref[0] * 256, 256)
    packed[pl.ds(mine, 256), :] = mine_ref[...]
    packed[pl.ds(256 - mine, 256), :] = other_ref[...]
    full[0:128, 0:128] = packed[0:128, :]
    full[0:128, 128:256] = packed[128:256, :]
    full[128:256, 0:128] = packed[128:256, :].T
    full[128:256, 128:256] = packed[256:384, :]
    full[256:288, 0:128] = packed[384:416, :]
    full[256:288, 128:256] = packed[416:448, :]
    full[256:288, 256:288] = packed[448:480, 0:32]
    strip = packed[384:448, :].T
    full[0:128, 256:288] = strip[:, 0:32]
    full[128:256, 256:288] = strip[:, 32:64]
    gram = full[...]
    statistic = stat_decay * prev_ref[...] + (1.0 - stat_decay) * gram
    stat_ref[...] = statistic
    norm = jnp.sqrt(jnp.sum(statistic * statistic, keepdims=True))
    row = lax.broadcasted_iota(jnp.int32, (BLOCK, BLOCK), 0)
    column = lax.broadcasted_iota(jnp.int32, (BLOCK, BLOCK), 1)
    five = jnp.where(row == column, f32(5.0), f32(0.0))
    normed = start_gain * statistic / norm
    factor = jnp.sqrt(jnp.sqrt(start_gain / norm))
    step = (five - normed) * 0.25
    step_pair = split(step)
    squared = split(dot3(step_pair, step_pair, MUL))
    fourth = split(dot3(squared, squared, MUL))
    second = (five - dot3(fourth, split(normed), MUL)) * 0.25
    root = dot3(step_pair, split(second), MUL) * factor
    root_ref[...] = root
    moved = dot3(split(gram), split(root), MUL)
    square_ref[...] = jnp.broadcast_to(jnp.sum(moved * root, keepdims=True), (8, 128))


def find_root(core, mine, other, prev):
    square = jax.ShapeDtypeStruct((BLOCK, BLOCK), f32)
    return pl.pallas_call(
        root_kernel,
        in_specs=[sm(), vm(), vm(), vm()],
        out_specs=[vm()] * 3,
        out_shape=[square, square, jax.ShapeDtypeStruct((8, 128), f32)],
        scratch_shapes=[pltpu.VMEM((512, 128), f32), pltpu.VMEM((BLOCK, BLOCK), f32)],
        compiler_params=params(16),
        cost_estimate=cost(36 * BLOCK**3, BLOCK * BLOCK * 16),
        name="root",
    )(core, mine, other, prev)


def move_kernel(root_ref, *refs):
    out = refs[-1]
    root = split(root_ref[...])
    place = 0
    for ref in refs[:-1]:
        rows = ref.shape[1]
        out[:, place : place + rows] = dot3(root, split(ref[...]), MUL)
        place += rows


def move(root, lives, rows):
    return pl.pallas_call(
        move_kernel,
        in_specs=[vm()] * (1 + len(lives)),
        out_specs=vm(),
        out_shape=jax.ShapeDtypeStruct((BLOCK, rows), f32),
        compiler_params=params(16),
        cost_estimate=cost(6 * BLOCK * BLOCK * rows, BLOCK * rows * 8),
        name="move",
    )(root, *lives)


def shards(grad_parts, embedding, stat_prev, row_flags):
    grad = pltpu.with_memory_space_constraint(grad_parts[0], pltpu.HBM)
    shard_rows = grad.shape[0]
    dp = lax.axis_index("dp")
    vocab = lax.axis_index("vocab")
    y, z = dp // 4, dp % 4
    x, core = (vocab // 2) % 4, vocab % 2
    put = lambda value, pairs: lax.ppermute(value, "dp", pairs)
    vput = lambda value, pairs: lax.ppermute(value, "vocab", pairs)
    mask = (row_flags > 0).astype(f32)[None, :]
    y_at = [jnp.reshape((y + step) % 4, (1,)) for step in range(4)]
    z_at = jnp.stack([z ^ flip for flip in range(4)])
    x_to = jnp.stack([(x + step) % 4 for step in range(4)])
    x_from = jnp.stack([(x - step) % 4 for step in range(4)])
    core_at = jnp.reshape(core, (1,))

    y_to = jnp.concatenate(y_at)
    where = jnp.concatenate([y_to, z_at])
    came, crossed = {}, {}
    base, crossing = where, None
    for step in range(COUNT + 2):
        if step == 5:
            where, crossed["side"] = lax.optimization_barrier((where, crossed["side"]))
        elif step == 7:
            where, crossed[0] = lax.optimization_barrier((where, crossed[0]))
        outs = run_step(step, grad, where, came, crossing)
        where, outs = lax.optimization_barrier((where, outs))
        came[step] = (put(outs[0], y_move(1)), put(outs[1], y_move(-1)))
        what, turned = PLAN.get(step, (None, 0))
        if turned == 1:
            crossing = [*outs[3:], put(outs[2], z_flip(1))]
        elif turned == 2:
            crossed[what] = [outs[2], put(outs[3], z_flip(2))]
    sent, first = {}, {}
    for number in (4, 5, 6):
        if number == 6:
            where, crossed[2], first[4] = lax.optimization_barrier((where, crossed[2], first[4]))
        sent[number] = cut(number, grad, where, came)
        first[number] = put(sent[number][0], z_flip(1))
    y_last, sent[6] = lax.optimization_barrier((y_to, sent[6]))
    side_pieces = side_cut(y_last, *crossed.pop("side"))
    tail = [side_pieces[0]] + [put(side_pieces[turned], y_move(turned)) for turned in (1, 2, 3)]
    for number in (4, 5, 6):
        if number == 6:
            first[6], crossed[4] = lax.optimization_barrier((first[6], crossed[4]))
        kept, leaves = mix(sent[number][1], first[number])
        crossed[number] = [kept, put(leaves, z_flip(2))]
    lives, prior = [], None
    place = 0
    for number in sorted(crossed):
        rows = crossed[number][0].shape[1]
        here = mask[:, place : place + rows]
        place += rows
        if number < 4:
            here, crossed[COUNT - 1][0] = lax.optimization_barrier((here, crossed[COUNT - 1][0]))
        if place < COUNT * ROWS:
            live, prior = finish(here, crossed[number], prior)
        else:
            side_live, prior = finish(mask[:, COUNT * ROWS :], tail, prior)
            live, keep, send = last(here, core_at, crossed[number], prior, ROWS)
        lives.append(live)
    lives.append(side_live)

    came = vput(send, v_move(0, 0, 1))
    quarters = quarter(x_to, keep, came)
    part = quarters[0]
    for step in (1, 2, 3):
        part = part + vput(quarters[step], v_move(0, step, 0))
    part = part + vput(part, v_move(1, 0, 0))
    parts = [part] + [vput(part, v_move(0, step, 0)) for step in (1, 2, 3)]
    mine = gather(x_from, parts)
    other = vput(mine, v_move(0, 0, 1))
    statistic, root, square = find_root(core_at, mine, other, stat_prev[0])

    total = square
    for step in (1, 2, 3):
        total = total + put(square, y_move(step))
    squares = total
    for flip in (1, 2, 3):
        squares = squares + put(total, z_flip(flip))
    direction = move(root, lives, shard_rows)
    entries = shard_rows * lax.axis_size("vocab") * BLOCK * lax.axis_size("dp")
    root_mean = jnp.sqrt(squares[0:1, 0:1] / entries + rms_epsilon)
    held = embedding.T
    stepped = (1.0 - learn_rate * weight_decay) * held - learn_rate * direction / root_mean
    updated = jnp.where(mask > 0, stepped, held).T
    panel = BLOCK // lax.axis_size("vocab")
    root_rows = lax.dynamic_slice_in_dim(root, vocab * panel, panel, 0)
    return (updated, statistic[None], root_rows[None])


def solution(mesh):
    placed = (P("dp", "vocab", None), P("vocab", "dp"), P("dp", None, None), P("vocab"))
    return jax.shard_map(
        shards,
        mesh=mesh,
        in_specs=placed,
        out_specs=(P("vocab", "dp"), P("dp", None, None), P("dp", "vocab", None)),
        check_vma=False,
    )
```

```python
import functools

import jax
import jax.numpy as jnp
from jax import lax
from jax.experimental import pallas as pl
from jax.experimental.pallas import tpu as pltpu
from jax.sharding import PartitionSpec as P

BLOCK = 288
HALF = 144
ROWS = 128
COUNT = 7
LIMIT = 20

stat_decay = 0.8
learn_rate = 0.5
weight_decay = 0.1
rms_epsilon = 1e-06
start_gain = 2.5
f32 = jnp.float32
bf16 = jnp.bfloat16

ANY_T = (((1,), (1,)), ((), ()))
MUL = (((1,), (0,)), ((), ()))


def params(mib):
    return pltpu.CompilerParams(vmem_limit_bytes=mib * 2**20)


def cost(flops, moved):
    return pl.CostEstimate(flops=int(flops), bytes_accessed=int(moved), transcendentals=0)


def vm():
    return pl.BlockSpec(memory_space=pltpu.VMEM)


def hbm():
    return pl.BlockSpec(memory_space=pltpu.HBM)


def sm():
    return pl.BlockSpec(memory_space=pltpu.SMEM)


def y_move(step):
    return [(y * 4 + z, ((y + step) % 4) * 4 + z) for y in range(4) for z in range(4)]


def z_flip(mask):
    return [(y * 4 + z, y * 4 + (z ^ mask)) for y in range(4) for z in range(4)]


def v_move(dh, dx, dc):
    pairs = []
    for h in range(2):
        for x in range(4):
            for c in range(2):
                to = (((h + dh) % 2) * 4 + (x + dx) % 4) * 2 + (c + dc) % 2
                pairs.append(((h * 4 + x) * 2 + c, to))
    return pairs


def split(value):
    high = value.astype(bf16)
    low = (value - high.astype(f32)).astype(bf16)
    return high, low


def dot3(left, right, dims):
    (a, b), (c, d) = left, right
    one = lambda p, q: lax.dot_general(p, q, dims, preferred_element_type=f32)
    return one(a, c) + (one(a, d) + one(b, c))


def turn(grad_ref, held):
    for tile in range(9):
        place = tile * 128
        held[place : place + 128, :] = grad_ref[:, place : place + 128].astype(f32).T


def fetch(grad_ref, block, sem, number, column):
    column = pl.multiple_of(column * 1152, 128)
    rows = pl.ds(number * ROWS, ROWS)
    copy = pltpu.make_async_copy(grad_ref.at[rows, pl.ds(column, 1152)], block, sem)
    copy.start()
    return copy


def slots(step):
    return (2 if step < COUNT else 0) + (1 if 0 <= step - 2 < COUNT else 0)


PLAN = {0: ("side", 1), 3: ("side", 2), 5: (0, 1), 6: (0, 2), 7: (2, 1), 8: (2, 2)}


def blocks_of(step):
    count = 3 * (step < COUNT) + 2 * (0 <= step - 2 < COUNT)
    if step in PLAN:
        what, turned = PLAN[step]
        count += 4 if what == "side" else 2 * (turned == 1)
    return count


def halves(k):
    first = pl.ds(pl.multiple_of(k * BLOCK, 16), HALF)
    second = pl.ds(pl.multiple_of(k * BLOCK + HALF, 16), HALF)
    return first, second


def step_kernel(step, at_ref, grad_ref, *refs):
    refs = list(refs)
    held, blocks, sems = refs[-3:]
    count = 2 + (2 if step in PLAN and PLAN[step] != ("side", 1) else step in PLAN)
    given, (up, down, *outs) = refs[: -3 - count], refs[-3 - count : -3]
    copies = []

    def order(number, column):
        place = len(copies)
        copies.append(fetch(grad_ref, blocks.at[place], sems.at[place], number, column))

    if step < COUNT:
        order(step, at_ref[2])
        order(step, at_ref[1])
        order(step, at_ref[3])
    if 0 <= step - 2 < COUNT:
        order(step - 2, at_ref[1])
        order(step - 2, at_ref[3])
    what, turned = PLAN.get(step, (None, 0))
    if what == "side":
        for y in range(4):
            order(COUNT, y)
    elif turned == 1:
        for i in range(2):
            order(what + i, at_ref[0])
    taken = []

    def take():
        place = len(taken)
        copies[place].wait()
        taken.append(place)
        turn(blocks.at[place], held)

    whole = [k * BLOCK for k in range(4)]
    if step < COUNT:
        take()
        for k in range(4):
            up[0, k] = held[whole[k] : whole[k] + HALF, :]
            down[0, k] = held[whole[k] + HALF : whole[k] + BLOCK, :]
        take()
        for k in range(4):
            up[1, k] = held[whole[k] + HALF : whole[k] + BLOCK, :]
        take()
        for k in range(4):
            down[1, k] = held[whole[k] : whole[k] + HALF, :]
    if 0 <= step - 2 < COUNT:
        came_up, came_down = given[:2]
        given = given[2:]
        slot = slots(step) - 1
        take()
        for k in range(4):
            up[slot, k] = held[whole[k] : whole[k] + HALF, :] + came_up[0, k]
        take()
        for k in range(4):
            down[slot, k] = held[whole[k] + HALF : whole[k] + BLOCK, :] + came_down[0, k]
    if what == "side":
        for y in range(4):
            take()
            for place in range(2):
                k = at_ref[4 + (place * 2 + (turned == 1))]
                part = held[pl.ds(pl.multiple_of(k * BLOCK, 16), BLOCK), :]
                if turned == 1:
                    outs[0][place, y] = part
                else:
                    outs[place][y] = part + given[0][place, y]
    elif turned == 1:
        for i in range(2):
            take()
            lanes = slice(i * ROWS, (i + 1) * ROWS)
            share(at_ref, held, given[4 * i : 4 * i + 4], slots(what + i + 2) - 1, outs[0], outs[1], lanes)
    elif turned == 2:
        for place in range(2):
            outs[place][...] = given[0][place] + given[1][place]


def scratch(count):
    return [
        pltpu.VMEM((1152, ROWS), f32),
        pltpu.VMEM((count, ROWS, 1152), bf16),
        pltpu.SemaphoreType.DMA((count,)),
    ]


def run_step(step, grad, where, came, crossing):
    given = list(came[step - 2]) if 0 <= step - 2 < COUNT else []
    shape = lambda *dims: jax.ShapeDtypeStruct(dims, f32)
    shapes = [shape(slots(step), 4, HALF, ROWS)] * 2
    what, turned = PLAN.get(step, (None, 0))
    if what == "side":
        shapes += [shape(2, 4, BLOCK, ROWS)] if turned == 1 else [shape(4, BLOCK, ROWS)] * 2
    elif turned == 1:
        for number in (what, what + 1):
            given += list(came[number]) + list(came[number + 2])
        shapes += [shape(2, BLOCK, 2 * ROWS)] * 2
    elif turned == 2:
        shapes += [shape(BLOCK, 2 * ROWS)] * 2
    if turned == 2:
        given += crossing
    return pl.pallas_call(
        functools.partial(step_kernel, step),
        in_specs=[sm(), hbm()] + [vm()] * len(given),
        out_specs=[vm()] * len(shapes),
        out_shape=shapes,
        scratch_shapes=scratch(blocks_of(step)),
        compiler_params=params(LIMIT),
        cost_estimate=cost(0, 22e6 * max(slots(step), 1)),
        name="step",
    )(where, grad, *given)


def share(at_ref, held, came, slot, leaves, stays, lanes):
    direct_up, direct_down, sum_up, sum_down = came
    for place in range(4):
        k = at_ref[4 + place]
        out = (stays, leaves)[place % 2]
        first, second = halves(k)
        out[place // 2, 0:HALF, lanes] = held[first, :] + (sum_up[slot, k] + direct_down[1, k])
        out[place // 2, HALF:BLOCK, lanes] = held[second, :] + (sum_down[slot, k] + direct_up[1, k])


def cut_kernel(number, at_ref, grad_ref, *refs):
    came, (leaves, stays, held, blocks, sems) = refs[:4], refs[4:]
    copy = fetch(grad_ref, blocks.at[0], sems.at[0], number, at_ref[0])
    copy.wait()
    turn(blocks.at[0], held)
    share(at_ref, held, came, slots(number + 2) - 1, leaves, stays, slice(0, ROWS))


def cut(number, grad, where, came):
    return pl.pallas_call(
        functools.partial(cut_kernel, number),
        in_specs=[sm(), hbm()] + [vm()] * 4,
        out_specs=[vm()] * 2,
        out_shape=[jax.ShapeDtypeStruct((2, BLOCK, ROWS), f32)] * 2,
        scratch_shapes=scratch(1),
        compiler_params=params(LIMIT),
        cost_estimate=cost(0, ROWS * 1152 * 20),
        name="cut",
    )(where, grad, *came[number], *came[number + 2])


def mix_kernel(stays, came, kept, leaves):
    kept[...] = stays[0] + came[0]
    leaves[...] = stays[1] + came[1]


def mix(stays, came):
    return pl.pallas_call(
        mix_kernel,
        in_specs=[vm()] * 2,
        out_specs=[vm()] * 2,
        out_shape=[jax.ShapeDtypeStruct((BLOCK, ROWS), f32)] * 2,
        compiler_params=params(LIMIT),
        cost_estimate=cost(0, ROWS * 1152 * 6),
        name="mix",
    )(stays, came)


def side_cut_kernel(y_ref, kept, part, *outs):
    for step in range(4):
        outs[step][...] = kept[y_ref[step]] + part[y_ref[step]]


def side_cut(y_to, kept, part):
    return pl.pallas_call(
        side_cut_kernel,
        in_specs=[sm(), vm(), vm()],
        out_specs=[vm()] * 4,
        out_shape=[jax.ShapeDtypeStruct((BLOCK, ROWS), f32)] * 4,
        compiler_params=params(LIMIT),
        cost_estimate=cost(0, 1152 * ROWS * 8),
        name="side_cut",
    )(y_to, kept, part)


def pack(full, ref):
    ref[0:128, :] = full[0:128, 0:128]
    ref[128:256, :] = full[0:128, 128:256]
    ref[256:384, :] = full[128:256, 128:256]
    ref[384:416, :] = full[256:288, 0:128]
    ref[416:448, :] = full[256:288, 128:256]
    ref[448:480, 0:32] = full[256:288, 256:288]


def finish_kernel(count, mask_ref, *refs):
    parts, prior, (live_ref, gram_ref) = refs[:count], refs[count:-2], refs[-2:]
    live = sum_of(parts) * mask_ref[...]
    live_ref[...] = live
    pair = split(live)
    gram = dot3(pair, pair, ANY_T)
    gram_ref[...] = gram + prior[0][...] if prior else gram


def sum_of(refs):
    if len(refs) == 2:
        return refs[0][...] + refs[1][...]
    return (refs[0][...] + refs[1][...]) + (refs[2][...] + refs[3][...])


def finish(mask, parts, prior):
    prior = [] if prior is None else [prior]
    rows = parts[0].shape[1]
    return pl.pallas_call(
        functools.partial(finish_kernel, len(parts)),
        in_specs=[vm()] * (1 + len(parts) + len(prior)),
        out_specs=[vm()] * 2,
        out_shape=[
            jax.ShapeDtypeStruct((BLOCK, rows), f32),
            jax.ShapeDtypeStruct((BLOCK, BLOCK), f32),
        ],
        compiler_params=params(16),
        cost_estimate=cost(6 * BLOCK * BLOCK * rows, BLOCK * rows * 24),
        name="finish",
    )(mask, *parts, *prior)


def last_kernel(mask_ref, core_ref, p0, p1, prior, live_ref, keep_ref, send_ref, packed):
    live = (p0[...] + p1[...]) * mask_ref[...]
    live_ref[...] = live
    pair = split(live)
    packed[...] = jnp.zeros_like(packed)
    pack(dot3(pair, pair, ANY_T) + prior[...], packed)
    mine = pl.multiple_of(core_ref[0] * 256, 256)
    keep_ref[...] = packed[pl.ds(mine, 256), :]
    send_ref[...] = packed[pl.ds(256 - mine, 256), :]


def last(mask, core, parts, prior, rows):
    return pl.pallas_call(
        last_kernel,
        in_specs=[vm(), sm()] + [vm()] * 3,
        out_specs=[vm()] * 3,
        out_shape=[
            jax.ShapeDtypeStruct((BLOCK, rows), f32),
            jax.ShapeDtypeStruct((256, 128), f32),
            jax.ShapeDtypeStruct((256, 128), f32),
        ],
        scratch_shapes=[pltpu.VMEM((512, 128), f32)],
        compiler_params=params(16),
        cost_estimate=cost(6 * BLOCK * BLOCK * rows, BLOCK * rows * 24),
        name="last",
    )(mask, core, *parts, prior)


def quarter_kernel(x_ref, keep, came, *outs):
    for step in range(4):
        at = pl.ds(pl.multiple_of(x_ref[step] * 64, 64), 64)
        outs[step][...] = keep[at, :] + came[at, :]


def quarter(x_at, keep, came):
    return pl.pallas_call(
        quarter_kernel,
        in_specs=[sm(), vm(), vm()],
        out_specs=[vm()] * 4,
        out_shape=[jax.ShapeDtypeStruct((64, 128), f32)] * 4,
        cost_estimate=cost(256 * 128, 256 * 128 * 12),
        compiler_params=params(8),
        name="quarter",
    )(x_at, keep, came)


def gather_kernel(x_ref, q0, q1, q2, q3, out):
    for step, ref in enumerate((q0, q1, q2, q3)):
        at = pl.ds(pl.multiple_of(x_ref[step] * 64, 64), 64)
        out[at, :] = ref[...]


def gather(x_from, parts):
    return pl.pallas_call(
        gather_kernel,
        in_specs=[sm()] + [vm()] * 4,
        out_specs=vm(),
        out_shape=jax.ShapeDtypeStruct((256, 128), f32),
        cost_estimate=cost(0, 256 * 128 * 8),
        compiler_params=params(8),
        name="gather",
    )(x_from, *parts)


def root_kernel(core_ref, mine_ref, other_ref, prev_ref, stat_ref, root_ref, square_ref, packed, full):
    mine = pl.multiple_of(core_ref[0] * 256, 256)
    packed[pl.ds(mine, 256), :] = mine_ref[...]
    packed[pl.ds(256 - mine, 256), :] = other_ref[...]
    full[0:128, 0:128] = packed[0:128, :]
    full[0:128, 128:256] = packed[128:256, :]
    full[128:256, 0:128] = packed[128:256, :].T
    full[128:256, 128:256] = packed[256:384, :]
    full[256:288, 0:128] = packed[384:416, :]
    full[256:288, 128:256] = packed[416:448, :]
    full[256:288, 256:288] = packed[448:480, 0:32]
    strip = packed[384:448, :].T
    full[0:128, 256:288] = strip[:, 0:32]
    full[128:256, 256:288] = strip[:, 32:64]
    gram = full[...]
    statistic = stat_decay * prev_ref[...] + (1.0 - stat_decay) * gram
    stat_ref[...] = statistic
    norm = jnp.sqrt(jnp.sum(statistic * statistic, keepdims=True))
    row = lax.broadcasted_iota(jnp.int32, (BLOCK, BLOCK), 0)
    column = lax.broadcasted_iota(jnp.int32, (BLOCK, BLOCK), 1)
    five = jnp.where(row == column, f32(5.0), f32(0.0))
    normed = start_gain * statistic / norm
    factor = jnp.sqrt(jnp.sqrt(start_gain / norm))
    step = (five - normed) * 0.25
    step_pair = split(step)
    squared = split(dot3(step_pair, step_pair, MUL))
    fourth = split(dot3(squared, squared, MUL))
    second = (five - dot3(fourth, split(normed), MUL)) * 0.25
    root = dot3(step_pair, split(second), MUL) * factor
    root_ref[...] = root
    moved = dot3(split(gram), split(root), MUL)
    square_ref[...] = jnp.broadcast_to(jnp.sum(moved * root, keepdims=True), (8, 128))


def find_root(core, mine, other, prev):
    square = jax.ShapeDtypeStruct((BLOCK, BLOCK), f32)
    return pl.pallas_call(
        root_kernel,
        in_specs=[sm(), vm(), vm(), vm()],
        out_specs=[vm()] * 3,
        out_shape=[square, square, jax.ShapeDtypeStruct((8, 128), f32)],
        scratch_shapes=[pltpu.VMEM((512, 128), f32), pltpu.VMEM((BLOCK, BLOCK), f32)],
        compiler_params=params(16),
        cost_estimate=cost(36 * BLOCK**3, BLOCK * BLOCK * 16),
        name="root",
    )(core, mine, other, prev)


def move_kernel(root_ref, *refs):
    out = refs[-1]
    root = split(root_ref[...])
    place = 0
    for ref in refs[:-1]:
        rows = ref.shape[1]
        out[:, place : place + rows] = dot3(root, split(ref[...]), MUL)
        place += rows


def move(root, lives, rows):
    return pl.pallas_call(
        move_kernel,
        in_specs=[vm()] * (1 + len(lives)),
        out_specs=vm(),
        out_shape=jax.ShapeDtypeStruct((BLOCK, rows), f32),
        compiler_params=params(16),
        cost_estimate=cost(6 * BLOCK * BLOCK * rows, BLOCK * rows * 8),
        name="move",
    )(root, *lives)


def update_kernel(entries, s0, s1, s2, s3, direction, held, mask, out):
    squares = (s0[0:1, 0:1] + s1[0:1, 0:1]) + (s2[0:1, 0:1] + s3[0:1, 0:1])
    scale = learn_rate / jnp.sqrt(squares / entries + rms_epsilon)
    live = jnp.broadcast_to(mask[...], (96, mask.shape[1])) > 0
    for place in range(0, BLOCK, 96):
        rows = slice(place, place + 96)
        kept = held[rows, :]
        stepped = (1.0 - learn_rate * weight_decay) * kept - direction[rows, :] * scale
        out[rows, :] = jnp.where(live, stepped, kept)


def update(entries, squares, direction, held, mask):
    return pl.pallas_call(
        functools.partial(update_kernel, entries),
        in_specs=[vm()] * 7,
        out_specs=vm(),
        out_shape=jax.ShapeDtypeStruct(held.shape, f32),
        compiler_params=params(16),
        cost_estimate=cost(0, 4 * held.size * 4),
        name="update",
    )(*squares, direction, held, mask)


def shards(grad_parts, embedding, stat_prev, row_flags):
    grad = pltpu.with_memory_space_constraint(grad_parts[0], pltpu.HBM)
    shard_rows = grad.shape[0]
    dp = lax.axis_index("dp")
    vocab = lax.axis_index("vocab")
    y, z = dp // 4, dp % 4
    x, core = (vocab // 2) % 4, vocab % 2
    put = lambda value, pairs: lax.ppermute(value, "dp", pairs)
    vput = lambda value, pairs: lax.ppermute(value, "vocab", pairs)
    mask = (row_flags > 0).astype(f32)[None, :]
    y_at = [jnp.reshape((y + step) % 4, (1,)) for step in range(4)]
    z_at = jnp.stack([z ^ flip for flip in range(4)])
    x_to = jnp.stack([(x + step) % 4 for step in range(4)])
    x_from = jnp.stack([(x - step) % 4 for step in range(4)])
    core_at = jnp.reshape(core, (1,))

    y_to = jnp.concatenate(y_at)
    where = jnp.concatenate([y_to, z_at])
    came, crossed = {}, {}
    base, crossing = where, None
    for step in range(COUNT + 2):
        if step == 5:
            where, crossed["side"] = lax.optimization_barrier((where, crossed["side"]))
        elif step == 7:
            where, crossed[0] = lax.optimization_barrier((where, crossed[0]))
        outs = run_step(step, grad, where, came, crossing)
        where, outs = lax.optimization_barrier((where, outs))
        came[step] = (put(outs[0], y_move(1)), put(outs[1], y_move(-1)))
        what, turned = PLAN.get(step, (None, 0))
        if turned == 1:
            crossing = [*outs[3:], put(outs[2], z_flip(1))]
        elif turned == 2:
            crossed[what] = [outs[2], put(outs[3], z_flip(2))]
    sent, first = {}, {}
    for number in (4, 5, 6):
        if number == 6:
            where, crossed[2], first[4] = lax.optimization_barrier((where, crossed[2], first[4]))
        sent[number] = cut(number, grad, where, came)
        first[number] = put(sent[number][0], z_flip(1))
    y_last, sent[6] = lax.optimization_barrier((y_to, sent[6]))
    side_pieces = side_cut(y_last, *crossed.pop("side"))
    tail = [side_pieces[0]] + [put(side_pieces[turned], y_move(turned)) for turned in (1, 2, 3)]
    for number in (4, 5, 6):
        if number == 6:
            first[6], crossed[4] = lax.optimization_barrier((first[6], crossed[4]))
        kept, leaves = mix(sent[number][1], first[number])
        crossed[number] = [kept, put(leaves, z_flip(2))]
    lives, prior = [], None
    place = 0
    for number in sorted(crossed):
        rows = crossed[number][0].shape[1]
        here = mask[:, place : place + rows]
        place += rows
        if number < 4:
            here, crossed[COUNT - 1][0] = lax.optimization_barrier((here, crossed[COUNT - 1][0]))
        if place < COUNT * ROWS:
            live, prior = finish(here, crossed[number], prior)
        else:
            side_live, prior = finish(mask[:, COUNT * ROWS :], tail, prior)
            live, keep, send = last(here, core_at, crossed[number], prior, ROWS)
        lives.append(live)
    lives.append(side_live)

    came = vput(send, v_move(0, 0, 1))
    quarters = quarter(x_to, keep, came)
    part = quarters[0]
    for step in (1, 2, 3):
        part = part + vput(quarters[step], v_move(0, step, 0))
    part = part + vput(part, v_move(1, 0, 0))
    parts = [part] + [vput(part, v_move(0, step, 0)) for step in (1, 2, 3)]
    mine = gather(x_from, parts)
    other = vput(mine, v_move(0, 0, 1))
    statistic, root, square = find_root(core_at, mine, other, stat_prev[0])

    total = square
    for step in (1, 2, 3):
        total = total + put(square, y_move(step))
    squares = [total] + [put(total, z_flip(flip)) for flip in (1, 2, 3)]
    direction = move(root, lives, shard_rows)
    entries = shard_rows * lax.axis_size("vocab") * BLOCK * lax.axis_size("dp")
    updated = update(entries, squares, direction, embedding.T, mask).T
    panel = BLOCK // lax.axis_size("vocab")
    root_rows = lax.dynamic_slice_in_dim(root, vocab * panel, panel, 0)
    return (updated, statistic[None], root_rows[None])


def solution(mesh):
    placed = (P("dp", "vocab", None), P("vocab", "dp"), P("dp", None, None), P("vocab"))
    return jax.shard_map(
        shards,
        mesh=mesh,
        in_specs=placed,
        out_specs=(P("vocab", "dp"), P("dp", None, None), P("dp", "vocab", None)),
        check_vma=False,
    )
```
